512 devices in a mesh: dp: 32 (over x, z), rep: 16 (over y, core).
Axes of the slice: x: 4, y: 8, z: 8, core: 2. Of those that a mesh axis runs over, the one named last changes fastest.
Arguments:
- layer_rows: bfloat16 [34816, 3584], P(('rep', 'dp')), parts along dimension 0, may hold values from -500 to 500
- norm_gain: float32 [3584], replicated, may hold values from 0.1 to 1.9
- w_gate: bfloat16 [3584, 9216], P(None, 'dp'), may hold values from -0.09375 to 0.09375
- req_len: int32 [1024], P('rep'), parts along dimension 0, may hold values from 1 to 67, as said below
- req_rank: int32 [1024], P('rep'), parts along dimension 0, may hold values from 0 to 31
Outputs:
- activated: bfloat16 [34816, 9216], P(('rep', 'dp')), parts along dimension 0
The draws below stay inside these ranges and needn't reach their ends.
There are 16 independent parts, one for each index of `rep`. The reference program is written for one: setup_inputs(seed, part) draws one part's arguments, and reference() takes and returns one part's arrays. A program takes and returns all parts, laid end to end along the dimension named above; an argument that names none is the same for every part. Nothing has to cross between parts.
Inputs may be any that keep to these rules, and one draw needn't show every extreme that they name: `req_len`: each rank owns exactly 2 requests. The lengths add up to 2048. The requests of one rank hold at most 68 rows, and one rank holds exactly 68; one request has exactly 67 rows.
All inputs are finite; a program needn't handle non-finite values.
Results may differ from the reference program's by a relative error of at most 0.005.
Values may be sent and summed in bfloat16 or wider, within the bound.
No kernel may reach another device: no remote copies, remote signals or barrier semaphores. Data moves between devices by JAX's collectives and lax.ppermute only.
A program may use at most 128 MiB of HBM per device.

```python
import math
import jax
import jax.numpy as jnp
from jax import lax

D = 3584
FF = 9216
TOK_DEV = 64
REQ_DEV = 2
CAP = 68
N_DP = 32


def request_table(key):
    pair_count = N_DP // 2
    spread_max = CAP - TOK_DEV
    offsets = jax.random.randint(jax.random.fold_in(key, 101), (pair_count,), 0, spread_max + 1)
    forced_pair = jax.random.randint(jax.random.fold_in(key, 102), (), 0, pair_count)
    offsets = jnp.where(jnp.arange(pair_count) == forced_pair, spread_max, offsets)
    side_bits = jax.random.randint(jax.random.fold_in(key, 103), (pair_count,), 0, 2)
    high_count = TOK_DEV + offsets
    low_count = TOK_DEV - offsets
    first_side = jnp.where(side_bits == 1, high_count, low_count)
    second_side = jnp.where(side_bits == 1, low_count, high_count)
    pair_counts = jnp.stack([first_side, second_side], axis=1).reshape(N_DP)
    rank_order = jax.random.permutation(jax.random.fold_in(key, 104), N_DP)
    rank_counts = pair_counts[rank_order]
    split_weights = jax.random.randint(jax.random.fold_in(key, 105), (N_DP, REQ_DEV), 1, 9)
    extra_rows = rank_counts - REQ_DEV
    shares = extra_rows[:, None] * split_weights // jnp.sum(split_weights, axis=1, keepdims=True)
    full_rank = rank_counts == CAP
    shares = jnp.where(full_rank[:, None], 0, shares)
    shares = shares.at[:, REQ_DEV - 1].add(extra_rows - jnp.sum(shares, axis=1))
    lengths = (1 + shares).reshape(N_DP * REQ_DEV)
    owners = jnp.repeat(jnp.arange(N_DP), REQ_DEV)
    request_order = jax.random.permutation(jax.random.fold_in(key, 106), N_DP * REQ_DEV)
    return (lengths[request_order].astype(jnp.int32), owners[request_order].astype(jnp.int32))


def draw_req_len(key, part):
    lengths, owners = request_table(key)
    return lengths


def draw_req_rank(key, part):
    lengths, owners = request_table(key)
    return owners


def draw_layer_rows(key, part):
    key = jax.random.fold_in(key, 3)
    base_key = jax.random.fold_in(key, 11)
    column_key = jax.random.fold_in(key, 12)
    row_key = jax.random.fold_in(key, 13)
    column_scale = jnp.exp(jax.random.uniform(column_key, (1, D), jnp.float32, 0.0, math.log(10.0)))
    row_scale = jnp.exp(jax.random.uniform(row_key, (N_DP * CAP, 1), jnp.float32, 0.0, math.log(10.0)))
    base = jnp.clip(jax.random.normal(base_key, (N_DP * CAP, D), jnp.float32), -5.0, 5.0)
    return (base * column_scale * row_scale).astype(jnp.bfloat16)


def steps_of(own_key, shape, split, least, high):
    def one(axis_at, blocks):
        heights = jax.random.uniform(jax.random.fold_in(jax.random.fold_in(own_key, 6), axis_at), (blocks,), jnp.float32, least / len(split), high / len(split))
        return jnp.repeat(jnp.exp(heights), shape[axis_at] // blocks).reshape((-1,) + (1,) * (len(shape) - axis_at - 1))

    loudness = one(*split[0])
    for cut in split[1:]:
        loudness = loudness * one(*cut)
    return loudness


def gaussian(stream_key, dims, deviation, bound, shards=(), kind=jnp.bfloat16):
    array = jax.random.normal(stream_key, dims, jnp.float32) * deviation
    if len(shards) > 0:
        array = steps_of(stream_key, dims, shards, -0.22, 0.18) * array
    return jnp.clip(array, min=-bound, max=bound).astype(kind)


def setup_inputs(seed: int = 0, part: int = 0) -> dict:
    streams_of = jax.random.split(jax.random.key(seed), 6)
    own_keys = jax.random.split(jax.random.fold_in(streams_of[5], part), 6)
    layer_rows = draw_layer_rows(jax.random.fold_in(jax.random.fold_in(streams_of[5], part), 71), part)
    norm_gain = jnp.clip(1.0 + 0.18 * jax.random.normal(streams_of[1], (D,), jnp.float32), 0.1, 1.9)
    w_gate = gaussian(streams_of[2], (D, FF), D ** -0.5, 0.09375, ((1, 32),))
    req_len = draw_req_len(jax.random.fold_in(jax.random.fold_in(streams_of[5], part), 71), part)
    req_rank = draw_req_rank(jax.random.fold_in(jax.random.fold_in(streams_of[5], part), 71), part)
    return {"layer_rows": layer_rows, "norm_gain": norm_gain, "w_gate": w_gate, "req_len": req_len, "req_rank": req_rank}


def reference(layer_rows, norm_gain, w_gate, req_len, req_rank):
    rank_ids = jnp.arange(N_DP, dtype=jnp.int32)
    member = (req_rank[:, None] == rank_ids[None, :]).astype(jnp.int32)
    counts = lax.optimization_barrier(jnp.sum(member * req_len[:, None], axis=0))
    slot_ids = jnp.arange(N_DP * CAP, dtype=jnp.int32)
    owner_rank = slot_ids // CAP
    within = slot_ids - owner_rank * CAP
    live_mask = within < counts[owner_rank]
    wide_rows = layer_rows.astype(jnp.float32)
    mean_square = lax.optimization_barrier(jnp.mean(wide_rows * wide_rows, axis=-1, keepdims=True))
    scaled = wide_rows * lax.rsqrt(mean_square + 1e-06) * norm_gain
    normed = jnp.where(live_mask[:, None], scaled, jnp.zeros((), jnp.float32)).astype(jnp.bfloat16)
    return jax.nn.silu(jnp.dot(normed, w_gate, preferred_element_type=jnp.float32)).astype(jnp.bfloat16)
```

```python
import jax
import jax.numpy as jnp
from jax import lax
from jax.experimental import pallas as pl
from jax.experimental.pallas import tpu as pltpu
from jax.sharding import Mesh
from jax.sharding import PartitionSpec as P

AXES = {"x": 4, "z": 8, "y": 8, "core": 2}
PAD = 80
MIB = 1024 * 1024


def hop(value, axes, move):
    sizes = [AXES[a] for a in axes]
    total = 1
    for s in sizes:
        total *= s
    pairs = []
    for source in range(total):
        rest, at = source, []
        for s in reversed(sizes):
            at.append(rest % s)
            rest //= s
        target = 0
        for s, c in zip(sizes, move(*reversed(at))):
            target = target * s + c % s
        pairs.append((source, target))
    return lax.ppermute(value, tuple(axes), pairs)


def along_z(value):
    return hop(value, ("z", "core"), lambda z, c: (z + 1 - 2 * c, c))


def along_y(value):
    return hop(value, ("y", "core"), lambda y, c: (y + 1 - 2 * c, c))


def along_x(value):
    return hop(value, ("x", "core"), lambda x, c: (x + 1 - 2 * c, c))


def other_core(value):
    return hop(value, ("core",), lambda c: (1 - c,))


def normalize(place, layer_rows, norm_gain, req_len, req_rank, after):
    rows, features = layer_rows.shape

    def body(place_ref, rows_ref, gain_ref, len_ref, rank_ref, after_ref, out):
        owned = jnp.where(rank_ref[...] == place_ref[4], len_ref[...], 0)
        live = lax.broadcasted_iota(jnp.int32, (rows, 1), 0) < jnp.sum(owned, axis=1, keepdims=True)
        wide = rows_ref[...].astype(jnp.float32)
        mean_square = jnp.mean(wide * wide, axis=-1, keepdims=True)
        scaled = wide * lax.rsqrt(mean_square + 1e-06) * gain_ref[...]
        out[...] = jnp.where(live, scaled, 0.0).astype(jnp.bfloat16)

    in_vmem = pl.BlockSpec(memory_space=pltpu.VMEM)
    return pl.pallas_call(
        body,
        out_shape=jax.ShapeDtypeStruct((rows, features), jnp.bfloat16),
        in_specs=[pl.BlockSpec(memory_space=pltpu.SMEM)] + [in_vmem] * 4 + [pl.BlockSpec(memory_space=pl.ANY)],
        out_specs=in_vmem,
        compiler_params=pltpu.CompilerParams(vmem_limit_bytes=8 * MIB),
        cost_estimate=pl.CostEstimate(flops=5 * rows * features, bytes_accessed=4 * rows * features, transcendentals=rows),
        name="normalize",
    )(place, layer_rows, norm_gain.reshape(1, -1), req_len.reshape(1, -1), req_rank.reshape(1, -1), after)


def line_up(place, pair, beside, far, swapped):
    rows, features = pair.shape[1:]

    def body(place_ref, pair_ref, beside_ref, far_ref, swapped_ref, out):
        x, c = place_ref[0], place_ref[1]
        back = 2 * c - 1

        def put(step, core, block):
            owner = lax.rem(x + step + 4, 4) * 2 + core
            out[pl.ds(pl.multiple_of(owner * PAD, 16), rows), :] = block

        put(0, c, pair_ref[0])
        put(0, 1 - c, pair_ref[1])
        put(back, c, beside_ref[0])
        put(back, 1 - c, beside_ref[1])
        put(2, c, far_ref[0])
        put(-back, 1 - c, swapped_ref[0])
        put(-back, c, swapped_ref[1])
        put(2, 1 - c, swapped_ref[2])

    return pl.pallas_call(
        body,
        out_shape=jax.ShapeDtypeStruct((8 * PAD, features), pair.dtype),
        in_specs=[pl.BlockSpec(memory_space=pltpu.SMEM)] + [pl.BlockSpec(memory_space=pltpu.VMEM)] * 4,
        out_specs=pl.BlockSpec(memory_space=pltpu.VMEM),
        compiler_params=pltpu.CompilerParams(vmem_limit_bytes=12 * MIB),
        cost_estimate=pl.CostEstimate(flops=0, bytes_accessed=32 * rows * features, transcendentals=0),
        name="line_up",
    )(place, pair, beside, far, swapped)


def project(place, rows_in, near, far, rows, after=()):
    total, features = rows_in.shape
    half = features // 2
    owners = total // PAD
    widths = [w.shape[0] for w in near]
    columns = sum(widths)
    given = list(near) + [w for w in far if w is not None]
    per = 2
    block = per * PAD

    def body(place_ref, a_ref, *refs):
        out = refs[-1]
        q = place_ref[2]
        first = pl.multiple_of(q * half, 128)
        second = pl.multiple_of((1 - q) * half, 128)
        a_first, a_second = a_ref[:, pl.ds(first, half)], a_ref[:, pl.ds(second, half)]
        w_first, w_second, rest = [], [], list(refs[len(near) : len(given)])
        for ref, other in zip(refs[: len(near)], far):
            if other is None:
                w_first.append(ref[:, pl.ds(first, half)])
                w_second.append(ref[:, pl.ds(second, half)])
            else:
                w_first.append(ref[...])
                w_second.append(rest.pop(0)[...])
        contract = (((1,), (1,)), ((), ()))
        gate = lax.dot_general(a_first, jnp.concatenate(w_first, 0), contract, preferred_element_type=jnp.float32)
        gate += lax.dot_general(a_second, jnp.concatenate(w_second, 0), contract, preferred_element_type=jnp.float32)
        act = (gate / (1.0 + jnp.exp(-gate))).astype(jnp.bfloat16)
        for i in range(per):
            out[i] = act[i * PAD : i * PAD + rows]

    return pl.pallas_call(
        body,
        grid=(owners // per,),
        out_shape=jax.ShapeDtypeStruct((owners, rows, columns), jnp.bfloat16),
        in_specs=[pl.BlockSpec(memory_space=pltpu.SMEM), pl.BlockSpec((block, features), lambda i: (i, 0))]
        + [pl.BlockSpec(w.shape, lambda i: (0, 0)) for w in given]
        + [pl.BlockSpec(memory_space=pl.ANY)] * len(after),
        out_specs=pl.BlockSpec((per, rows, columns), lambda i: (i, 0, 0)),
        compiler_params=pltpu.CompilerParams(vmem_limit_bytes=20 * MIB),
        cost_estimate=pl.CostEstimate(
            flops=2 * total * features * columns,
            bytes_accessed=2 * (total * features + features * columns + total * columns),
            transcendentals=total * columns,
        ),
        name="project",
    )(place, rows_in, *given, *after)


def settle(place, early, late, width):
    rows = early.shape[1]
    half = width // 2
    region = 8 * width

    def body(place_ref, early_ref, late_ref, out):
        z = place_ref[3]

        def take(ref, core, k, n=1):
            return ref[core, :, k * half : (k + n) * half]

        def flipped(ref, k):
            return [take(ref, 1, k + 1), take(ref, 1, k)]

        parts = [take(late_ref, 0, 0, 2), take(early_ref, 0, 3, 2), take(early_ref, 0, 1, 2)]
        parts += [take(early_ref, 0, 0), take(early_ref, 1, 0)]
        parts += flipped(early_ref, 1) + flipped(early_ref, 3) + flipped(late_ref, 0)
        parts += [take(late_ref, 0, 2), take(late_ref, 1, 2)]
        line = jnp.concatenate([p.astype(jnp.float32) for p in parts], axis=1)
        line = pltpu.roll(line, lax.rem(z + 5, 8) * width, 1)
        out[...] = line.astype(jnp.bfloat16)

    return pl.pallas_call(
        body,
        grid=(4,),
        out_shape=jax.ShapeDtypeStruct((rows, 4 * region), jnp.bfloat16),
        in_specs=[pl.BlockSpec(memory_space=pltpu.SMEM)]
        + [pl.BlockSpec((2, rows, g.shape[2]), lambda i: (i, 0, 0)) for g in (early, late)],
        out_specs=pl.BlockSpec((rows, region), lambda i: (0, i)),
        compiler_params=pltpu.CompilerParams(vmem_limit_bytes=20 * MIB),
        cost_estimate=pl.CostEstimate(flops=0, bytes_accessed=16 * rows * region, transcendentals=0),
        name="settle",
    )(place, early, late)


def shards(layer_rows, norm_gain, w_gate, req_len, req_rank):
    x, z, y, c = (lax.axis_index(a) for a in ("x", "z", "y", "core"))
    rows, features = layer_rows.shape
    width = w_gate.shape[1]
    half_width, half = width // 2, features // 2
    plane = lax.rem(y, 2)
    place = jnp.stack([x, c, plane, z, x * AXES["z"] + z]).astype(jnp.int32)

    weights = w_gate.T

    def own(core):
        return lax.dynamic_slice(weights, (core * half_width, plane * half), (half_width, half))

    together = lax.optimization_barrier
    a, b = [own(c)], [own(1 - c)]
    a.append(along_z(a[0]))
    b.append(along_z(b[0]))

    normed = normalize(place, layer_rows, norm_gain, req_len, req_rank, a[0])
    pair = jnp.stack([normed, other_core(normed)])
    pair, a[1] = together((pair, a[1]))
    beside = along_x(pair)
    a.append(along_z(a[1]))
    b.append(along_z(b[1]))
    near1 = [jnp.concatenate([a[1], b[1]], 0)]
    far1 = [along_y(near1[0])]
    onward, a[2], b[1] = together((beside[:1], a[2], b[1]))
    far = along_x(onward)
    a.append(along_z(a[2]))
    b.append(along_z(b[2]))
    near1.append(jnp.concatenate([a[2], b[2]], 0))
    far1.append(along_y(near1[1]))
    others, b[2], far1[0] = together((jnp.concatenate([beside, far], 0), b[2], far1[0]))
    swapped = other_core(others)
    a[3], far1[0] = together((a[3], far1[0]))
    a.append(along_z(a[3]))
    rows_in = line_up(place, pair, beside, far, swapped)

    own_half = lax.dynamic_slice(weights, (c * half_width, 0), (half_width, features))
    first = project(place, rows_in, [own_half] + near1, [None] + far1, rows)
    early = lax.all_to_all(first, ("x", "core"), 0, 0, tiled=True)
    a[4], first = together((a[4], first))
    near2 = [a[3], b[3], a[4]]
    far2 = [along_y(w) for w in near2]
    far2[0], early = together((far2[0], early))
    second = project(place, rows_in, near2, far2, rows, after=(first,))
    late = lax.all_to_all(second, ("x", "core"), 0, 0, tiled=True)
    return settle(place, early, late, width)


def solution(mesh):
    grid = Mesh(mesh.devices.reshape(tuple(AXES.values())), tuple(AXES))
    rows = P(("y", "core", "x", "z"), None)
    in_specs = (rows, P(), P(None, ("x", "z")), P(("y", "core")), P(("y", "core")))
    return jax.shard_map(shards, mesh=grid, in_specs=in_specs, out_specs=rows, check_vma=False)
```

```python
import jax
import jax.numpy as jnp
from jax import lax
from jax.experimental import pallas as pl
from jax.experimental.pallas import tpu as pltpu
from jax.sharding import Mesh
from jax.sharding import PartitionSpec as P

AXES = {"x": 4, "z": 8, "y": 8, "core": 2}
PAD = 80
MIB = 1024 * 1024
TINY = pl.CostEstimate(flops=0, bytes_accessed=1024, transcendentals=0)


def hop(value, axes, move):
    sizes = [AXES[a] for a in axes]
    total = 1
    for s in sizes:
        total *= s
    pairs = []
    for source in range(total):
        rest, at = source, []
        for s in reversed(sizes):
            at.append(rest % s)
            rest //= s
        target = 0
        for s, c in zip(sizes, move(*reversed(at))):
            target = target * s + c % s
        pairs.append((source, target))
    return lax.ppermute(value, tuple(axes), pairs)


def along_z(value):
    return hop(value, ("z", "core"), lambda z, c: (z + 1 - 2 * c, c))


def along_y(value):
    return hop(value, ("y", "core"), lambda y, c: (y + 1 - 2 * c, c))


def along_x(value):
    return hop(value, ("x", "core"), lambda x, c: (x + 1 - 2 * c, c))


def other_core(value):
    return hop(value, ("core",), lambda c: (1 - c,))


def after(value, *others):
    return lax.optimization_barrier((value, *others))[0]


def normalize(place, layer_rows, norm_gain, req_len, req_rank):
    rows, features = layer_rows.shape

    def body(place_ref, rows_ref, gain_ref, len_ref, rank_ref, out):
        owned = jnp.where(rank_ref[...] == place_ref[4], len_ref[...], 0)
        live = lax.broadcasted_iota(jnp.int32, (rows, 1), 0) < jnp.sum(owned, axis=1, keepdims=True)
        wide = rows_ref[...].astype(jnp.float32)
        mean_square = jnp.mean(wide * wide, axis=-1, keepdims=True)
        scaled = wide * lax.rsqrt(mean_square + 1e-06) * gain_ref[...]
        out[...] = jnp.where(live, scaled, 0.0).astype(jnp.bfloat16)

    in_vmem = pl.BlockSpec(memory_space=pltpu.VMEM)
    return pl.pallas_call(
        body,
        out_shape=jax.ShapeDtypeStruct((rows, features), jnp.bfloat16),
        in_specs=[pl.BlockSpec(memory_space=pltpu.SMEM)] + [in_vmem] * 4,
        out_specs=in_vmem,
        compiler_params=pltpu.CompilerParams(vmem_limit_bytes=8 * MIB),
        cost_estimate=TINY,
        name="normalize",
    )(place, layer_rows, norm_gain.reshape(1, -1), req_len.reshape(1, -1), req_rank.reshape(1, -1))


def line_up(place, pair, beside, far, swapped, across):
    rows, features = pair.shape[1:]

    def body(place_ref, pair_ref, beside_ref, far_ref, swapped_ref, across_ref, out):
        x, c = place_ref[0], place_ref[1]
        back = 2 * c - 1

        def put(step, core, block):
            owner = lax.rem(x + step + 4, 4) * 2 + core
            out[pl.ds(pl.multiple_of(owner * PAD, 16), rows), :] = block

        put(0, c, pair_ref[0])
        put(0, 1 - c, pair_ref[1])
        put(back, c, beside_ref[0])
        put(back, 1 - c, beside_ref[1])
        put(2, c, far_ref[0])
        put(-back, 1 - c, swapped_ref[0])
        put(-back, c, swapped_ref[1])
        put(2, 1 - c, across_ref[0])

    return pl.pallas_call(
        body,
        out_shape=jax.ShapeDtypeStruct((8 * PAD, features), pair.dtype),
        in_specs=[pl.BlockSpec(memory_space=pltpu.SMEM)] + [pl.BlockSpec(memory_space=pltpu.VMEM)] * 5,
        out_specs=pl.BlockSpec(memory_space=pltpu.VMEM),
        compiler_params=pltpu.CompilerParams(vmem_limit_bytes=12 * MIB),
        cost_estimate=TINY,
        name="line_up",
    )(place, pair, beside, far, swapped, across)


def project(place, rows_in, near, far, rows):
    total, features = rows_in.shape
    half = features // 2
    owners = total // PAD
    widths = [w.shape[0] for w in near]
    columns = sum(widths)
    given = list(near) + [w for w in far if w is not None]
    per = 4
    block = per * PAD

    def body(place_ref, a_ref, *refs):
        out = refs[-1]
        q = place_ref[2]
        first = pl.multiple_of(q * half, 128)
        second = pl.multiple_of((1 - q) * half, 128)
        a_first, a_second = a_ref[:, pl.ds(first, half)], a_ref[:, pl.ds(second, half)]
        w_first, w_second, rest = [], [], list(refs[len(near) : len(given)])
        for ref, other in zip(refs[: len(near)], far):
            if other is None:
                w_first.append(ref[:, pl.ds(first, half)])
                w_second.append(ref[:, pl.ds(second, half)])
            else:
                w_first.append(ref[...])
                w_second.append(rest.pop(0)[...])
        contract = (((1,), (1,)), ((), ()))
        gate = lax.dot_general(a_first, jnp.concatenate(w_first, 0), contract, preferred_element_type=jnp.float32)
        gate += lax.dot_general(a_second, jnp.concatenate(w_second, 0), contract, preferred_element_type=jnp.float32)
        act = (gate / (1.0 + jnp.exp(-gate))).astype(jnp.bfloat16)
        for i in range(per):
            out[i] = act[i * PAD : i * PAD + rows]

    return pl.pallas_call(
        body,
        grid=(owners // per,),
        out_shape=jax.ShapeDtypeStruct((owners, rows, columns), jnp.bfloat16),
        in_specs=[pl.BlockSpec(memory_space=pltpu.SMEM), pl.BlockSpec((block, features), lambda i: (i, 0))]
        + [pl.BlockSpec(w.shape, lambda i: (0, 0)) for w in given],
        out_specs=pl.BlockSpec((per, rows, columns), lambda i: (i, 0, 0)),
        compiler_params=pltpu.CompilerParams(vmem_limit_bytes=20 * MIB),
        cost_estimate=TINY,
        name="project",
    )(place, rows_in, *given)


def settle(place, early, late, width):
    rows = early.shape[1]
    half = width // 2
    region = 8 * width

    def body(place_ref, early_ref, late_ref, out):
        z = place_ref[3]

        def take(ref, core, k, n=1):
            return ref[core, :, k * half : (k + n) * half]

        def flipped(ref, k):
            return [take(ref, 1, k + 1), take(ref, 1, k)]

        parts = [take(late_ref, 0, 0, 2), take(early_ref, 0, 3, 2), take(early_ref, 0, 1, 2)]
        parts += [take(early_ref, 0, 0), take(early_ref, 1, 0)]
        parts += flipped(early_ref, 1) + flipped(early_ref, 3) + flipped(late_ref, 0)
        parts += [take(late_ref, 0, 2), take(late_ref, 1, 2)]
        line = jnp.concatenate([p.astype(jnp.float32) for p in parts], axis=1)
        line = pltpu.roll(line, lax.rem(z + 5, 8) * width, 1)
        out[...] = line.astype(jnp.bfloat16)

    return pl.pallas_call(
        body,
        grid=(4,),
        out_shape=jax.ShapeDtypeStruct((rows, 4 * region), jnp.bfloat16),
        in_specs=[pl.BlockSpec(memory_space=pltpu.SMEM)]
        + [pl.BlockSpec((2, rows, g.shape[2]), lambda i: (i, 0, 0)) for g in (early, late)],
        out_specs=pl.BlockSpec((rows, region), lambda i: (0, i)),
        compiler_params=pltpu.CompilerParams(vmem_limit_bytes=20 * MIB),
        cost_estimate=TINY,
        name="settle",
    )(place, early, late)


def shards(layer_rows, norm_gain, w_gate, req_len, req_rank):
    x, z, y, c = (lax.axis_index(a) for a in ("x", "z", "y", "core"))
    rows, features = layer_rows.shape
    width = w_gate.shape[1]
    half_width, half = width // 2, features // 2
    plane = lax.rem(y, 2)
    place = jnp.stack([x, c, plane, z, x * AXES["z"] + z]).astype(jnp.int32)

    weights = w_gate.T

    def own(core):
        return lax.dynamic_slice(weights, (core * half_width, plane * half), (half_width, half))

    a, b = [own(c)], [own(1 - c)]
    a.append(along_z(a[0]))
    b.append(along_z(b[0]))

    normed = normalize(place, layer_rows, after(norm_gain, a[0]), req_len, req_rank)
    pair = jnp.stack([normed, other_core(normed)])
    beside = along_x(pair)
    a.append(along_z(a[1]))
    b.append(along_z(b[1]))
    near = [jnp.concatenate([a[1], b[1]], 0)]
    far = [along_y(near[0])]
    swapped = other_core(beside)
    distant = along_x(after(beside[:1], a[2], b[2]))
    a.append(along_z(a[2]))
    b.append(along_z(b[2]))
    near.append(jnp.concatenate([a[2], b[2]], 0))
    far.append(along_y(near[1]))
    across = other_core(after(distant, a[3], b[3]))
    a.append(along_z(after(a[3], far[0])))
    far_a, far_b = along_y(a[3]), along_y(b[3])
    rows_in = line_up(place, pair, beside, distant, swapped, across)
    own_half = lax.dynamic_slice(weights, (c * half_width, 0), (half_width, features))

    def deliver(value):
        return lax.all_to_all(value, ("x", "core"), 0, 0, tiled=True)

    far_4 = along_y(a[4])
    first = project(place, after(rows_in, a[4], far_a), [own_half] + near, [None] + far, rows)
    early = deliver(first)
    second = project(place, after(rows_in, first), [a[3], b[3], a[4]], [far_a, far_b, far_4], rows)
    late = deliver(after(second, early))
    return settle(place, early, late, width)


def solution(mesh):
    grid = Mesh(mesh.devices.reshape(tuple(AXES.values())), tuple(AXES))
    rows = P(("y", "core", "x", "z"), None)
    in_specs = (rows, P(), P(None, ("x", "z")), P(("y", "core")), P(("y", "core")))
    return jax.shard_map(shards, mesh=grid, in_specs=in_specs, out_specs=rows, check_vma=False)
```

```python
import jax
import jax.numpy as jnp
from jax import lax
from jax.experimental import pallas as pl
from jax.experimental.pallas import tpu as pltpu
from jax.sharding import Mesh
from jax.sharding import PartitionSpec as P

AXES = {"x": 4, "z": 8, "y": 8, "core": 2}
PAD = 80
MIB = 1024 * 1024
TINY = pl.CostEstimate(flops=0, bytes_accessed=1024, transcendentals=0)


def hop(value, axes, move):
    sizes = [AXES[a] for a in axes]
    total = 1
    for s in sizes:
        total *= s
    pairs = []
    for source in range(total):
        rest, at = source, []
        for s in reversed(sizes):
            at.append(rest % s)
            rest //= s
        target = 0
        for s, c in zip(sizes, move(*reversed(at))):
            target = target * s + c % s
        pairs.append((source, target))
    return lax.ppermute(value, tuple(axes), pairs)


def along_z(value):
    return hop(value, ("z", "core"), lambda z, c: (z + 1 - 2 * c, c))


def along_y(value):
    return hop(value, ("y", "core"), lambda y, c: (y + 1 - 2 * c, c))


def along_x(value):
    return hop(value, ("x", "core"), lambda x, c: (x + 1 - 2 * c, c))


def other_core(value):
    return hop(value, ("core",), lambda c: (1 - c,))


def after(value, *others):
    return lax.optimization_barrier((value, *others))[0]


def normalize(place, layer_rows, norm_gain, req_len, req_rank):
    rows, features = layer_rows.shape

    def body(place_ref, rows_ref, gain_ref, len_ref, rank_ref, out):
        owned = jnp.where(rank_ref[...] == place_ref[4], len_ref[...], 0)
        live = lax.broadcasted_iota(jnp.int32, (rows, 1), 0) < jnp.sum(owned, axis=1, keepdims=True)
        wide = rows_ref[...].astype(jnp.float32)
        mean_square = jnp.mean(wide * wide, axis=-1, keepdims=True)
        scaled = wide * lax.rsqrt(mean_square + 1e-06) * gain_ref[...]
        out[...] = jnp.where(live, scaled, 0.0).astype(jnp.bfloat16)

    in_vmem = pl.BlockSpec(memory_space=pltpu.VMEM)
    return pl.pallas_call(
        body,
        out_shape=jax.ShapeDtypeStruct((rows, features), jnp.bfloat16),
        in_specs=[pl.BlockSpec(memory_space=pltpu.SMEM)] + [in_vmem] * 4,
        out_specs=in_vmem,
        compiler_params=pltpu.CompilerParams(vmem_limit_bytes=8 * MIB),
        cost_estimate=TINY,
        name="normalize",
    )(place, layer_rows, norm_gain.reshape(1, -1), req_len.reshape(1, -1), req_rank.reshape(1, -1))


def line_up(place, pair, beside, distant, swapped, across):
    rows, features = pair.shape[1:]

    def body(place_ref, pair_ref, beside_ref, distant_ref, swapped_ref, across_ref, out):
        x, c = place_ref[0], place_ref[1]
        back = 2 * c - 1

        def put(step, core, block):
            owner = lax.rem(x + step + 4, 4) * 2 + core
            out[pl.ds(pl.multiple_of(owner * PAD, 16), rows), :] = block

        put(0, c, pair_ref[0])
        put(0, 1 - c, pair_ref[1])
        put(back, c, beside_ref[0])
        put(back, 1 - c, beside_ref[1])
        put(2, c, distant_ref[0])
        put(-back, 1 - c, swapped_ref[0])
        put(-back, c, swapped_ref[1])
        put(2, 1 - c, across_ref[0])

    return pl.pallas_call(
        body,
        out_shape=jax.ShapeDtypeStruct((8 * PAD, features), pair.dtype),
        in_specs=[pl.BlockSpec(memory_space=pltpu.SMEM)] + [pl.BlockSpec(memory_space=pltpu.VMEM)] * 5,
        out_specs=pl.BlockSpec(memory_space=pltpu.VMEM),
        compiler_params=pltpu.CompilerParams(vmem_limit_bytes=12 * MIB),
        cost_estimate=TINY,
        name="line_up",
    )(place, pair, beside, distant, swapped, across)


def project(place, rows_in, near, far, rows, columns, into=None):
    total, features = rows_in.shape
    half = features // 2
    owners = total // PAD
    given = list(near) + [w for w in far if w is not None]
    made = sum(w.shape[0] for w in near)
    span = columns if into is None else -(-made // 128) * 128
    per = 4
    block = per * PAD

    def body(place_ref, a_ref, *refs):
        out, rest = refs[-1], list(refs[len(near) : len(given)])
        q = place_ref[2]
        first = pl.multiple_of(q * half, 128)
        second = pl.multiple_of((1 - q) * half, 128)
        here = pl.ds(pl.multiple_of(pl.program_id(0) * block, 16), block)
        a_first, a_second = a_ref[here, pl.ds(first, half)], a_ref[here, pl.ds(second, half)]
        w_first, w_second = [], []
        for ref, other in zip(refs[: len(near)], far):
            if other is None:
                w_first.append(ref[:, pl.ds(first, half)])
                w_second.append(ref[:, pl.ds(second, half)])
            else:
                w_first.append(ref[...])
                w_second.append(rest.pop(0)[...])
        contract = (((1,), (1,)), ((), ()))
        gate = lax.dot_general(a_first, jnp.concatenate(w_first, 0), contract, preferred_element_type=jnp.float32)
        gate += lax.dot_general(a_second, jnp.concatenate(w_second, 0), contract, preferred_element_type=jnp.float32)
        act = (gate / (1.0 + jnp.exp(-gate))).astype(jnp.bfloat16)
        if into is not None:
            out[...] = refs[len(given)][...]
        for i in range(per):
            out[i, :, :made] = act[i * PAD : i * PAD + rows]

    whole = pl.BlockSpec(memory_space=pltpu.VMEM)
    part = pl.BlockSpec((per, rows, span), lambda i: (i, 0, 0))
    kept = [] if into is None else [into]
    return pl.pallas_call(
        body,
        grid=(owners // per,),
        out_shape=jax.ShapeDtypeStruct((owners, rows, columns), jnp.bfloat16),
        in_specs=[pl.BlockSpec(memory_space=pltpu.SMEM)] + [whole] * (1 + len(given)) + [part] * len(kept),
        out_specs=part,
        input_output_aliases={2 + len(given): 0} if kept else {},
        compiler_params=pltpu.CompilerParams(vmem_limit_bytes=20 * MIB),
        cost_estimate=TINY,
        name="project",
    )(place, rows_in, *given, *kept)


def settle(place, received, width):
    rows = received.shape[1]
    half = width // 2
    region = 8 * width

    def body(place_ref, ref, out):
        z = place_ref[3]

        def take(core, k, n=1):
            return ref[core, :, k * half : (k + n) * half]

        parts = [take(0, 6, 2), take(0, 4, 2), take(0, 2, 2), take(0, 1), take(1, 1)]
        for k in (2, 4, 6):
            parts += [take(1, k + 1), take(1, k)]
        parts += [take(0, 0), take(1, 0)]
        line = jnp.concatenate([p.astype(jnp.float32) for p in parts], axis=1)
        line = pltpu.roll(line, lax.rem(z + 5, 8) * width, 1)
        out[...] = line.astype(jnp.bfloat16)

    return pl.pallas_call(
        body,
        grid=(4,),
        out_shape=jax.ShapeDtypeStruct((rows, 4 * region), jnp.bfloat16),
        in_specs=[
            pl.BlockSpec(memory_space=pltpu.SMEM),
            pl.BlockSpec((2, rows, received.shape[2]), lambda i: (i, 0, 0)),
        ],
        out_specs=pl.BlockSpec((rows, region), lambda i: (0, i)),
        compiler_params=pltpu.CompilerParams(vmem_limit_bytes=20 * MIB),
        cost_estimate=TINY,
        name="settle",
    )(place, received)


def shards(layer_rows, norm_gain, w_gate, req_len, req_rank):
    x, z, y, c = (lax.axis_index(a) for a in ("x", "z", "y", "core"))
    rows, features = layer_rows.shape
    width = w_gate.shape[1]
    half_width, half = width // 2, features // 2
    plane = lax.rem(y, 2)
    place = jnp.stack([x, c, plane, z, x * AXES["z"] + z]).astype(jnp.int32)

    weights = w_gate.T

    def own(core):
        return lax.dynamic_slice(weights, (core * half_width, plane * half), (half_width, half))

    a, b = [own(c)], [own(1 - c)]
    a.append(along_z(a[0]))
    b.append(along_z(b[0]))

    normed = normalize(place, layer_rows, after(norm_gain, a[0]), req_len, req_rank)
    pair = jnp.stack([normed, other_core(normed)])
    beside = along_x(pair)
    a.append(along_z(after(a[1], pair)))
    b.append(along_z(b[1]))
    near = [jnp.concatenate([a[1], b[1]], 0)]
    far = [along_y(near[0])]
    distant = along_x(after(beside[:1], a[2]))
    a.append(along_z(a[2]))
    b.append(along_z(after(b[2], beside)))
    near.append(jnp.concatenate([a[2], b[2]], 0))
    far.append(along_y(near[1]))
    a.append(along_z(after(a[3], far[0])))
    near += [a[3], b[3]]
    far += [along_y(a[3]), along_y(after(b[3], distant))]
    far_4 = along_y(after(a[4], far[1], far[2]))
    swapped, across = other_core(after(beside, a[3])), other_core(distant)
    rows_in = line_up(place, pair, beside, distant, swapped, across)

    columns = 4 * width
    own_half = lax.dynamic_slice(weights, (c * half_width, 0), (half_width, features))
    gate = project(place, after(rows_in, a[4]), [own_half, own_half] + near, [None, None] + far, rows, columns)
    gate = project(place, rows_in, a[4:], [far_4], rows, columns, gate)
    received = lax.all_to_all(gate, ("x", "core"), 0, 0, tiled=True)
    return settle(place, received, width)


def solution(mesh):
    grid = Mesh(mesh.devices.reshape(tuple(AXES.values())), tuple(AXES))
    rows = P(("y", "core", "x", "z"), None)
    in_specs = (rows, P(), P(None, ("x", "z")), P(("y", "core")), P(("y", "core")))
    return jax.shard_map(shards, mesh=grid, in_specs=in_specs, out_specs=rows, check_vma=False)
```

```python
import jax
import jax.numpy as jnp
from jax import lax
from jax.experimental import pallas as pl
from jax.experimental.pallas import tpu as pltpu
from jax.sharding import Mesh
from jax.sharding import PartitionSpec as P

AXES = {"x": 4, "z": 8, "y": 8, "core": 2}
PAD = 80
MIB = 1024 * 1024
TINY = pl.CostEstimate(flops=0, bytes_accessed=1024, transcendentals=0)


def hop(value, axes, move):
    sizes = [AXES[a] for a in axes]
    total = 1
    for s in sizes:
        total *= s
    pairs = []
    for source in range(total):
        rest, at = source, []
        for s in reversed(sizes):
            at.append(rest % s)
            rest //= s
        target = 0
        for s, c in zip(sizes, move(*reversed(at))):
            target = target * s + c % s
        pairs.append((source, target))
    return lax.ppermute(value, tuple(axes), pairs)


def along_z(value):
    return hop(value, ("z", "core"), lambda z, c: (z + 1 - 2 * c, c))


def along_y(value):
    return hop(value, ("y", "core"), lambda y, c: (y + 1 - 2 * c, c))


def along_x(value):
    return hop(value, ("x", "core"), lambda x, c: (x + 1 - 2 * c, c))


def other_core(value):
    return hop(value, ("core",), lambda c: (1 - c,))


def after(value, *others):
    return lax.optimization_barrier((value, *others))[0]


def mark(*seen):
    def body(*refs):
        refs[-1][...] = jnp.zeros_like(refs[-1])

    return pl.pallas_call(
        body,
        out_shape=jax.ShapeDtypeStruct((8, 128), jnp.float32),
        in_specs=[pl.BlockSpec(memory_space=pl.ANY)] * len(seen),
        out_specs=pl.BlockSpec(memory_space=pltpu.VMEM),
        compiler_params=pltpu.CompilerParams(has_side_effects=True),
        cost_estimate=pl.CostEstimate(flops=10**11, bytes_accessed=1024, transcendentals=0),
        name="mark",
    )(*seen)


def normalize(place, layer_rows, norm_gain, req_len, req_rank):
    rows, features = layer_rows.shape

    def body(place_ref, rows_ref, gain_ref, len_ref, rank_ref, out):
        owned = jnp.where(rank_ref[...] == place_ref[4], len_ref[...], 0)
        live = lax.broadcasted_iota(jnp.int32, (rows, 1), 0) < jnp.sum(owned, axis=1, keepdims=True)
        wide = rows_ref[...].astype(jnp.float32)
        mean_square = jnp.mean(wide * wide, axis=-1, keepdims=True)
        scaled = wide * lax.rsqrt(mean_square + 1e-06) * gain_ref[...]
        out[...] = jnp.where(live, scaled, 0.0).astype(jnp.bfloat16)

    in_vmem = pl.BlockSpec(memory_space=pltpu.VMEM)
    return pl.pallas_call(
        body,
        out_shape=jax.ShapeDtypeStruct((rows, features), jnp.bfloat16),
        in_specs=[pl.BlockSpec(memory_space=pltpu.SMEM)] + [in_vmem] * 4,
        out_specs=in_vmem,
        compiler_params=pltpu.CompilerParams(vmem_limit_bytes=8 * MIB),
        cost_estimate=TINY,
        name="normalize",
    )(place, layer_rows, norm_gain.reshape(1, -1), req_len.reshape(1, -1), req_rank.reshape(1, -1))


def line_up(place, pair, beside, distant, swapped, across):
    rows, features = pair.shape[1:]

    def body(place_ref, pair_ref, beside_ref, distant_ref, swapped_ref, across_ref, out):
        x, c = place_ref[0], place_ref[1]
        back = 2 * c - 1

        def put(step, core, block):
            owner = lax.rem(x + step + 4, 4) * 2 + core
            out[pl.ds(pl.multiple_of(owner * PAD, 16), rows), :] = block

        put(0, c, pair_ref[0])
        put(0, 1 - c, pair_ref[1])
        put(back, c, beside_ref[0])
        put(back, 1 - c, beside_ref[1])
        put(2, c, distant_ref[...])
        put(-back, 1 - c, swapped_ref[0])
        put(-back, c, swapped_ref[1])
        put(2, 1 - c, across_ref[...])

    return pl.pallas_call(
        body,
        out_shape=jax.ShapeDtypeStruct((8 * PAD, features), pair.dtype),
        in_specs=[pl.BlockSpec(memory_space=pltpu.SMEM)] + [pl.BlockSpec(memory_space=pltpu.VMEM)] * 5,
        out_specs=pl.BlockSpec(memory_space=pltpu.VMEM),
        compiler_params=pltpu.CompilerParams(vmem_limit_bytes=12 * MIB),
        cost_estimate=TINY,
        name="line_up",
    )(place, pair, beside, distant, swapped, across)


def project(place, rows_in, near, far, rows, columns, into=None):
    total, features = rows_in.shape
    half = features // 2
    owners = total // PAD
    given = list(near) + [w for w in far if w is not None]
    made = sum(w.shape[0] for w in near)
    span = columns if into is None else -(-made // 128) * 128
    per = 4
    block = per * PAD

    def body(place_ref, a_ref, *refs):
        out, rest = refs[-1], list(refs[len(near) : len(given)])
        q = place_ref[2]
        first = pl.multiple_of(q * half, 128)
        second = pl.multiple_of((1 - q) * half, 128)
        here = pl.ds(pl.multiple_of(pl.program_id(0) * block, 16), block)
        a_first, a_second = a_ref[here, pl.ds(first, half)], a_ref[here, pl.ds(second, half)]
        w_first, w_second = [], []
        for ref, other in zip(refs[: len(near)], far):
            if other is None:
                w_first.append(ref[:, pl.ds(first, half)])
                w_second.append(ref[:, pl.ds(second, half)])
            else:
                w_first.append(ref[...])
                w_second.append(rest.pop(0)[...])
        contract = (((1,), (1,)), ((), ()))
        gate = lax.dot_general(a_first, jnp.concatenate(w_first, 0), contract, preferred_element_type=jnp.float32)
        gate += lax.dot_general(a_second, jnp.concatenate(w_second, 0), contract, preferred_element_type=jnp.float32)
        act = (gate / (1.0 + jnp.exp(-gate))).astype(jnp.bfloat16)
        if into is not None:
            out[...] = refs[len(given)][...]
        for i in range(per):
            out[i, :, :made] = act[i * PAD : i * PAD + rows]

    whole = pl.BlockSpec(memory_space=pltpu.VMEM)
    part = pl.BlockSpec((per, rows, span), lambda i: (i, 0, 0))
    kept = [] if into is None else [into]
    return pl.pallas_call(
        body,
        grid=(owners // per,),
        out_shape=jax.ShapeDtypeStruct((owners, rows, columns), jnp.bfloat16),
        in_specs=[pl.BlockSpec(memory_space=pltpu.SMEM)] + [whole] * (1 + len(given)) + [part] * len(kept),
        out_specs=part,
        input_output_aliases={2 + len(given): 0} if kept else {},
        compiler_params=pltpu.CompilerParams(vmem_limit_bytes=20 * MIB),
        cost_estimate=TINY,
        name="project",
    )(place, rows_in, *given, *kept)


def settle(place, received, width):
    rows = received.shape[1]
    half = width // 2
    region = 8 * width

    def body(place_ref, ref, out):
        z = place_ref[3]

        def take(core, k, n=1):
            return ref[core, :, k * half : (k + n) * half]

        parts = [take(0, 6, 2), take(0, 4, 2), take(0, 2, 2), take(0, 1), take(1, 1)]
        for k in (2, 4, 6):
            parts += [take(1, k + 1), take(1, k)]
        parts += [take(0, 0), take(1, 0)]
        line = jnp.concatenate([p.astype(jnp.float32) for p in parts], axis=1)
        line = pltpu.roll(line, lax.rem(z + 5, 8) * width, 1)
        out[...] = line.astype(jnp.bfloat16)

    return pl.pallas_call(
        body,
        grid=(4,),
        out_shape=jax.ShapeDtypeStruct((rows, 4 * region), jnp.bfloat16),
        in_specs=[
            pl.BlockSpec(memory_space=pltpu.SMEM),
            pl.BlockSpec((2, rows, received.shape[2]), lambda i: (i, 0, 0)),
        ],
        out_specs=pl.BlockSpec((rows, region), lambda i: (0, i)),
        compiler_params=pltpu.CompilerParams(vmem_limit_bytes=20 * MIB),
        cost_estimate=TINY,
        name="settle",
    )(place, received)


def shards(layer_rows, norm_gain, w_gate, req_len, req_rank):
    x, z, y, c = (lax.axis_index(a) for a in ("x", "z", "y", "core"))
    rows, features = layer_rows.shape
    width = w_gate.shape[1]
    half_width, half = width // 2, features // 2
    plane = lax.rem(y, 2)
    place = jnp.stack([x, c, plane, z, x * AXES["z"] + z]).astype(jnp.int32)

    weights = w_gate.T

    def own(core):
        return lax.dynamic_slice(weights, (core * half_width, plane * half), (half_width, half))

    a, b = [own(c)], [own(1 - c)]
    a.append(along_z(a[0]))
    b.append(along_z(b[0]))
    normed = normalize(place, layer_rows, after(norm_gain, a[0]), req_len, req_rank)
    pair = jnp.stack([normed, other_core(normed)])
    point = mark(pair)
    beside = along_x(after(pair, point))
    point = mark(point, a[1])
    a.append(along_z(after(a[1], point)))
    point = mark(point, b[1])
    b.append(along_z(after(b[1], point)))
    near = [jnp.concatenate([a[1], after(b[1], point)], 0)]
    far = [along_y(near[0])]
    point = mark(point, a[2])
    a.append(along_z(after(a[2], point)))
    point = mark(point, beside)
    distant = along_x(after(beside[0], point))
    point = mark(point, b[2])
    b.append(along_z(after(b[2], point)))
    near.append(jnp.concatenate([a[2], after(b[2], point)], 0))
    far.append(along_y(near[1]))
    point = mark(point, a[3], far[0])
    a.append(along_z(after(a[3], point)))
    far.append(along_y(after(a[3], point)))
    point = mark(point, distant)
    swapped = other_core(after(beside, point))
    point = mark(point, b[3])
    far.append(along_y(after(b[3], point)))
    point = mark(point, swapped)
    across = other_core(after(distant, point))
    point = mark(point, a[4], far[1])
    far_4 = along_y(after(a[4], point))
    point = mark(point, across, far[2])
    near += [a[3], b[3]]
    rows_in = line_up(place, pair, beside, after(distant, point), swapped, across)

    columns = 4 * width
    own_half = lax.dynamic_slice(weights, (c * half_width, 0), (half_width, features))
    gate = project(place, rows_in, [own_half, own_half] + near, [None, None] + far, rows, columns)
    gate = project(place, rows_in, a[4:], [far_4], rows, columns, gate)
    received = lax.all_to_all(gate, ("x", "core"), 0, 0, tiled=True)
    return settle(place, received, width)


def solution(mesh):
    grid = Mesh(mesh.devices.reshape(tuple(AXES.values())), tuple(AXES))
    rows = P(("y", "core", "x", "z"), None)
    in_specs = (rows, P(), P(None, ("x", "z")), P(("y", "core")), P(("y", "core")))
    return jax.shard_map(shards, mesh=grid, in_specs=in_specs, out_specs=rows, check_vma=False)
```

```python
import jax
import jax.numpy as jnp
from jax import lax
from jax.experimental import pallas as pl
from jax.experimental.pallas import tpu as pltpu
from jax.sharding import Mesh
from jax.sharding import PartitionSpec as P

AXES = {"x": 4, "z": 8, "y": 8, "core": 2}
PAD = 80
MIB = 1024 * 1024
TINY = pl.CostEstimate(flops=0, bytes_accessed=1024, transcendentals=0)


def hop(value, axes, move):
    sizes = [AXES[a] for a in axes]
    total = 1
    for s in sizes:
        total *= s
    pairs = []
    for source in range(total):
        rest, at = source, []
        for s in reversed(sizes):
            at.append(rest % s)
            rest //= s
        target = 0
        for s, c in zip(sizes, move(*reversed(at))):
            target = target * s + c % s
        pairs.append((source, target))
    return lax.ppermute(value, tuple(axes), pairs)


def along_z(value):
    return hop(value, ("z", "core"), lambda z, c: (z + 1 - 2 * c, c))


def along_y(value):
    return hop(value, ("y", "core"), lambda y, c: (y + 1 - 2 * c, c))


def along_x(value):
    return hop(value, ("x", "core"), lambda x, c: (x + 1 - 2 * c, c))


def other_core(value):
    return hop(value, ("core",), lambda c: (1 - c,))


def after(value, *others):
    return lax.optimization_barrier((value, *others))[0]


def normalize(place, layer_rows, norm_gain, req_len, req_rank):
    rows, features = layer_rows.shape

    def body(place_ref, rows_ref, gain_ref, len_ref, rank_ref, out):
        owned = jnp.where(rank_ref[...] == place_ref[4], len_ref[...], 0)
        live = lax.broadcasted_iota(jnp.int32, (rows, 1), 0) < jnp.sum(owned, axis=1, keepdims=True)
        wide = rows_ref[...].astype(jnp.float32)
        mean_square = jnp.mean(wide * wide, axis=-1, keepdims=True)
        scaled = wide * lax.rsqrt(mean_square + 1e-06) * gain_ref[...]
        out[...] = jnp.where(live, scaled, 0.0).astype(jnp.bfloat16)

    in_vmem = pl.BlockSpec(memory_space=pltpu.VMEM)
    return pl.pallas_call(
        body,
        out_shape=jax.ShapeDtypeStruct((rows, features), jnp.bfloat16),
        in_specs=[pl.BlockSpec(memory_space=pltpu.SMEM)] + [in_vmem] * 4,
        out_specs=in_vmem,
        compiler_params=pltpu.CompilerParams(vmem_limit_bytes=8 * MIB),
        cost_estimate=TINY,
        name="normalize",
    )(place, layer_rows, norm_gain.reshape(1, -1), req_len.reshape(1, -1), req_rank.reshape(1, -1))


def line_up(gathered):
    owners, rows, features = gathered.shape

    def body(ref, out):
        for i in range(owners):
            out[i * PAD : i * PAD + rows, :] = ref[i]

    return pl.pallas_call(
        body,
        out_shape=jax.ShapeDtypeStruct((owners * PAD, features), gathered.dtype),
        in_specs=[pl.BlockSpec(memory_space=pltpu.VMEM)],
        out_specs=pl.BlockSpec(memory_space=pltpu.VMEM),
        compiler_params=pltpu.CompilerParams(vmem_limit_bytes=12 * MIB),
        cost_estimate=TINY,
        name="line_up",
    )(gathered)


def project(place, rows_in, near, far, rows, columns, into=None):
    total, features = rows_in.shape
    half = features // 2
    owners = total // PAD
    given = list(near) + [w for w in far if w is not None]
    made = sum(w.shape[0] for w in near)
    span = columns if into is None else -(-made // 128) * 128
    per = 4
    block = per * PAD

    def body(place_ref, a_ref, *refs):
        out, rest = refs[-1], list(refs[len(near) : len(given)])
        q = place_ref[2]
        first = pl.multiple_of(q * half, 128)
        second = pl.multiple_of((1 - q) * half, 128)
        here = pl.ds(pl.multiple_of(pl.program_id(0) * block, 16), block)
        a_first, a_second = a_ref[here, pl.ds(first, half)], a_ref[here, pl.ds(second, half)]
        w_first, w_second = [], []
        for ref, other in zip(refs[: len(near)], far):
            if other is None:
                w_first.append(ref[:, pl.ds(first, half)])
                w_second.append(ref[:, pl.ds(second, half)])
            else:
                w_first.append(ref[...])
                w_second.append(rest.pop(0)[...])
        contract = (((1,), (1,)), ((), ()))
        gate = lax.dot_general(a_first, jnp.concatenate(w_first, 0), contract, preferred_element_type=jnp.float32)
        gate += lax.dot_general(a_second, jnp.concatenate(w_second, 0), contract, preferred_element_type=jnp.float32)
        act = (gate / (1.0 + jnp.exp(-gate))).astype(jnp.bfloat16)
        if into is not None:
            out[...] = refs[len(given)][...]
        for i in range(per):
            out[i, :, :made] = act[i * PAD : i * PAD + rows]

    whole = pl.BlockSpec(memory_space=pltpu.VMEM)
    part = pl.BlockSpec((per, rows, span), lambda i: (i, 0, 0))
    kept = [] if into is None else [into]
    return pl.pallas_call(
        body,
        grid=(owners // per,),
        out_shape=jax.ShapeDtypeStruct((owners, rows, columns), jnp.bfloat16),
        in_specs=[pl.BlockSpec(memory_space=pltpu.SMEM)] + [whole] * (1 + len(given)) + [part] * len(kept),
        out_specs=part,
        input_output_aliases={2 + len(given): 0} if kept else {},
        compiler_params=pltpu.CompilerParams(vmem_limit_bytes=20 * MIB),
        cost_estimate=TINY,
        name="project",
    )(place, rows_in, *given, *kept)


def settle(place, received, width):
    rows = received.shape[1]
    half = width // 2
    region = 8 * width

    def body(place_ref, ref, out):
        z = place_ref[3]

        def take(core, k, n=1):
            return ref[core, :, k * half : (k + n) * half]

        parts = [take(0, 6, 2), take(0, 4, 2), take(0, 2, 2), take(0, 1), take(1, 1)]
        for k in (2, 4, 6):
            parts += [take(1, k + 1), take(1, k)]
        parts += [take(0, 0), take(1, 0)]
        line = jnp.concatenate([p.astype(jnp.float32) for p in parts], axis=1)
        line = pltpu.roll(line, lax.rem(z + 5, 8) * width, 1)
        out[...] = line.astype(jnp.bfloat16)

    return pl.pallas_call(
        body,
        grid=(4,),
        out_shape=jax.ShapeDtypeStruct((rows, 4 * region), jnp.bfloat16),
        in_specs=[
            pl.BlockSpec(memory_space=pltpu.SMEM),
            pl.BlockSpec((2, rows, received.shape[2]), lambda i: (i, 0, 0)),
        ],
        out_specs=pl.BlockSpec((rows, region), lambda i: (0, i)),
        compiler_params=pltpu.CompilerParams(vmem_limit_bytes=20 * MIB),
        cost_estimate=TINY,
        name="settle",
    )(place, received)


def shards(layer_rows, norm_gain, w_gate, req_len, req_rank):
    x, z, y, c = (lax.axis_index(a) for a in ("x", "z", "y", "core"))
    rows, features = layer_rows.shape
    width = w_gate.shape[1]
    half_width, half = width // 2, features // 2
    plane = lax.rem(y, 2)
    place = jnp.stack([x, c, plane, z, x * AXES["z"] + z]).astype(jnp.int32)

    weights = w_gate.T

    def own(core):
        return lax.dynamic_slice(weights, (core * half_width, plane * half), (half_width, half))

    a, b = [own(c)], [own(1 - c)]
    a.append(along_z(a[0]))
    b.append(along_z(b[0]))

    normed = normalize(place, layer_rows, after(norm_gain, a[0]), req_len, req_rank)
    copies = jnp.broadcast_to(normed, (8, rows, features))
    gathered = lax.all_to_all(copies, ("x", "core"), 0, 0, tiled=True)
    a.append(along_z(a[1]))
    b.append(along_z(b[1]))
    near = [jnp.concatenate([a[1], b[1]], 0)]
    far = [along_y(near[0])]
    a.append(along_z(a[2]))
    b.append(along_z(b[2]))
    near.append(jnp.concatenate([a[2], b[2]], 0))
    far.append(along_y(near[1]))
    a.append(along_z(after(a[3], far[0])))
    near += [a[3], b[3]]
    far += [along_y(a[3]), along_y(b[3])]
    far_4 = along_y(after(a[4], far[1], far[2]))
    rows_in = line_up(gathered)

    columns = 4 * width
    own_half = lax.dynamic_slice(weights, (c * half_width, 0), (half_width, features))
    gate = project(place, after(rows_in, a[4]), [own_half, own_half] + near, [None, None] + far, rows, columns)
    gate = project(place, rows_in, a[4:], [far_4], rows, columns, gate)
    received = lax.all_to_all(gate, ("x", "core"), 0, 0, tiled=True)
    return settle(place, received, width)


def solution(mesh):
    grid = Mesh(mesh.devices.reshape(tuple(AXES.values())), tuple(AXES))
    rows = P(("y", "core", "x", "z"), None)
    in_specs = (rows, P(), P(None, ("x", "z")), P(("y", "core")), P(("y", "core")))
    return jax.shard_map(shards, mesh=grid, in_specs=in_specs, out_specs=rows, check_vma=False)
```

```python
import jax
import jax.numpy as jnp
from jax import lax
from jax.experimental import pallas as pl
from jax.experimental.pallas import tpu as pltpu
from jax.sharding import Mesh
from jax.sharding import PartitionSpec as P

AXES = {"x": 4, "z": 8, "y": 8, "core": 2}
PAD = 80
MIB = 1024 * 1024
TINY = pl.CostEstimate(flops=0, bytes_accessed=1024, transcendentals=0)


def hop(value, axes, move):
    sizes = [AXES[a] for a in axes]
    total = 1
    for s in sizes:
        total *= s
    pairs = []
    for source in range(total):
        rest, at = source, []
        for s in reversed(sizes):
            at.append(rest % s)
            rest //= s
        target = 0
        for s, c in zip(sizes, move(*reversed(at))):
            target = target * s + c % s
        pairs.append((source, target))
    return lax.ppermute(value, tuple(axes), pairs)


def along_z(value):
    return hop(value, ("z", "core"), lambda z, c: (z + 1 - 2 * c, c))


def along_y(value):
    return hop(value, ("y", "core"), lambda y, c: (y + 1 - 2 * c, c))


def along_x(value):
    return hop(value, ("x", "core"), lambda x, c: (x + 1 - 2 * c, c))


def other_core(value):
    return hop(value, ("core",), lambda c: (1 - c,))


def after(value, *others):
    return lax.optimization_barrier((value, *others))[0]


def mark(*seen):
    def body(*refs):
        refs[-1][...] = jnp.zeros_like(refs[-1])

    return pl.pallas_call(
        body,
        out_shape=jax.ShapeDtypeStruct((8, 128), jnp.float32),
        in_specs=[pl.BlockSpec(memory_space=pltpu.VMEM)] * len(seen),
        out_specs=pl.BlockSpec(memory_space=pltpu.VMEM),
        compiler_params=pltpu.CompilerParams(has_side_effects=True, vmem_limit_bytes=8 * MIB),
        cost_estimate=pl.CostEstimate(flops=10**11, bytes_accessed=1024, transcendentals=0),
        name="mark",
    )(*seen)


def normalize(place, layer_rows, norm_gain, req_len, req_rank):
    rows, features = layer_rows.shape

    def body(place_ref, rows_ref, gain_ref, len_ref, rank_ref, out):
        owned = jnp.where(rank_ref[...] == place_ref[4], len_ref[...], 0)
        live = lax.broadcasted_iota(jnp.int32, (rows, 1), 0) < jnp.sum(owned, axis=1, keepdims=True)
        wide = rows_ref[...].astype(jnp.float32)
        mean_square = jnp.mean(wide * wide, axis=-1, keepdims=True)
        scaled = wide * lax.rsqrt(mean_square + 1e-06) * gain_ref[...]
        out[...] = jnp.where(live, scaled, 0.0).astype(jnp.bfloat16)

    in_vmem = pl.BlockSpec(memory_space=pltpu.VMEM)
    return pl.pallas_call(
        body,
        out_shape=jax.ShapeDtypeStruct((rows, features), jnp.bfloat16),
        in_specs=[pl.BlockSpec(memory_space=pltpu.SMEM)] + [in_vmem] * 4,
        out_specs=in_vmem,
        compiler_params=pltpu.CompilerParams(vmem_limit_bytes=8 * MIB),
        cost_estimate=TINY,
        name="normalize",
    )(place, layer_rows, norm_gain.reshape(1, -1), req_len.reshape(1, -1), req_rank.reshape(1, -1))


def line_up(place, pair, beside, distant, swapped):
    rows, features = pair.shape[1:]

    def body(place_ref, pair_ref, beside_ref, distant_ref, swapped_ref, out):
        x, c = place_ref[0], place_ref[1]
        back = 2 * c - 1

        def put(step, core, block):
            owner = lax.rem(x + step + 4, 4) * 2 + core
            out[pl.ds(pl.multiple_of(owner * PAD, 16), rows), :] = block

        put(0, c, pair_ref[0])
        put(0, 1 - c, pair_ref[1])
        put(back, c, beside_ref[0])
        put(back, 1 - c, beside_ref[1])
        put(2, c, distant_ref[0])
        put(-back, 1 - c, swapped_ref[0])
        put(-back, c, swapped_ref[1])
        put(2, 1 - c, swapped_ref[2])

    return pl.pallas_call(
        body,
        out_shape=jax.ShapeDtypeStruct((8 * PAD, features), pair.dtype),
        in_specs=[pl.BlockSpec(memory_space=pltpu.SMEM)] + [pl.BlockSpec(memory_space=pltpu.VMEM)] * 4,
        out_specs=pl.BlockSpec(memory_space=pltpu.VMEM),
        compiler_params=pltpu.CompilerParams(vmem_limit_bytes=12 * MIB),
        cost_estimate=TINY,
        name="line_up",
    )(place, pair, beside, distant, swapped)


def project(place, rows_in, near, far, rows, columns, start, lead, into=None):
    total, features = rows_in.shape
    half = features // 2
    owners = total // PAD
    given = list(near) + [w for w in far if w is not None]
    end = start + lead + sum(w.shape[0] for w in near)
    span = columns if into is None else -(-end // 128) * 128
    per = 4
    block = per * PAD

    def body(place_ref, a_ref, *refs):
        out, rest = refs[-1], list(refs[len(near) : len(given)])
        q = place_ref[2]
        first = pl.multiple_of(q * half, 128)
        second = pl.multiple_of((1 - q) * half, 128)
        here = pl.ds(pl.multiple_of(pl.program_id(0) * block, 16), block)
        a_first, a_second = a_ref[here, pl.ds(first, half)], a_ref[here, pl.ds(second, half)]
        w_first, w_second = [], []
        for ref, other in zip(refs[: len(near)], far):
            if other is None:
                w_first.append(ref[:, pl.ds(first, half)])
                w_second.append(ref[:, pl.ds(second, half)])
            else:
                w_first.append(ref[...])
                w_second.append(rest.pop(0)[...])
        if lead:
            w_first.insert(0, w_first[0][:lead])
            w_second.insert(0, w_second[0][:lead])
        contract = (((1,), (1,)), ((), ()))
        gate = lax.dot_general(a_first, jnp.concatenate(w_first, 0), contract, preferred_element_type=jnp.float32)
        gate += lax.dot_general(a_second, jnp.concatenate(w_second, 0), contract, preferred_element_type=jnp.float32)
        act = (gate / (1.0 + jnp.exp(-gate))).astype(jnp.bfloat16)
        if into is not None:
            out[...] = refs[len(given)][...]
        for i in range(per):
            out[i, :, start:end] = act[i * PAD : i * PAD + rows]

    whole = pl.BlockSpec(memory_space=pltpu.VMEM)
    part = pl.BlockSpec((per, rows, span), lambda i: (i, 0, 0))
    kept = [] if into is None else [into]
    return pl.pallas_call(
        body,
        grid=(owners // per,),
        out_shape=jax.ShapeDtypeStruct((owners, rows, columns), jnp.bfloat16),
        in_specs=[pl.BlockSpec(memory_space=pltpu.SMEM)] + [whole] * (1 + len(given)) + [part] * len(kept),
        out_specs=part,
        input_output_aliases={2 + len(given): 0} if kept else {},
        compiler_params=pltpu.CompilerParams(vmem_limit_bytes=20 * MIB),
        cost_estimate=TINY,
        name="project",
    )(place, rows_in, *given, *kept)


def settle(place, received, width):
    rows = received.shape[1]
    half = width // 2
    region = 8 * width

    def body(place_ref, ref, out):
        z = place_ref[3]

        def take(core, k, n=1):
            return ref[core, :, k * half : (k + n) * half]

        parts = [take(0, 1, 2), take(0, 6, 2), take(0, 4, 2), take(0, 3), take(1, 3)]
        for k in (4, 6, 1):
            parts += [take(1, k + 1), take(1, k)]
        parts += [take(0, 0), take(1, 0)]
        line = jnp.concatenate([p.astype(jnp.float32) for p in parts], axis=1)
        line = pltpu.roll(line, lax.rem(z + 5, 8) * width, 1)
        out[...] = line.astype(jnp.bfloat16)

    return pl.pallas_call(
        body,
        grid=(4,),
        out_shape=jax.ShapeDtypeStruct((rows, 4 * region), jnp.bfloat16),
        in_specs=[
            pl.BlockSpec(memory_space=pltpu.SMEM),
            pl.BlockSpec((2, rows, received.shape[2]), lambda i: (i, 0, 0)),
        ],
        out_specs=pl.BlockSpec((rows, region), lambda i: (0, i)),
        compiler_params=pltpu.CompilerParams(vmem_limit_bytes=20 * MIB),
        cost_estimate=TINY,
        name="settle",
    )(place, received)


def shards(layer_rows, norm_gain, w_gate, req_len, req_rank):
    x, z, y, c = (lax.axis_index(a) for a in ("x", "z", "y", "core"))
    rows, features = layer_rows.shape
    width = w_gate.shape[1]
    half_width, half = width // 2, features // 2
    plane = lax.rem(y, 2)
    place = jnp.stack([x, c, plane, z, x * AXES["z"] + z]).astype(jnp.int32)

    weights = w_gate.T

    def own(core):
        return lax.dynamic_slice(weights, (core * half_width, plane * half), (half_width, half))

    a, b = [own(c)], [own(1 - c)]
    a.append(along_z(a[0]))
    b.append(along_z(b[0]))
    normed = normalize(place, layer_rows, after(norm_gain, a[0]), req_len, req_rank)
    pair = jnp.stack([normed, other_core(normed)])
    beside = along_x(pair)

    a.append(along_z(a[1]))
    point = mark(a[1])
    b[1] = after(b[1], point)
    b.append(along_z(b[1]))
    near = [jnp.concatenate([a[1], b[1]], 0)]
    far = [along_y(near[0])]

    a.append(along_z(a[2]))
    point = mark(point, a[2], beside)
    distant = along_x(after(beside[:1], point))
    b[2] = after(b[2], point)
    b.append(along_z(b[2]))
    near.append(jnp.concatenate([a[2], b[2]], 0))
    far.append(along_y(near[1]))

    a.append(along_z(a[3]))
    point = mark(point, a[3], distant, far[0])
    swapped = other_core(after(jnp.concatenate([beside, distant], 0), point))
    near += [a[3], b[3]]
    far += [along_y(after(a[3], point)), along_y(after(b[3], point))]

    near.append(a[4])
    far.append(along_y(a[4]))
    point = mark(point, a[4], far[1])
    rows_in = line_up(place, pair, beside, after(distant, point), swapped)

    own_half = lax.dynamic_slice(weights, (c * half_width, 0), (half_width, features))
    columns = 4 * width
    begin = half_width * 3 // 128 * 128
    gate = project(
        place, rows_in, [own_half] + near[:2], [None] + far[:2], rows, columns, begin, half_width * 3 - begin
    )
    begin = half_width // 128 * 128
    gate = project(place, rows_in, near[2:4], far[2:4], rows, columns, begin, half_width - begin, gate)
    gate = project(place, rows_in, near[4:], far[4:], rows, columns, 0, 0, gate)
    received = lax.all_to_all(gate, ("x", "core"), 0, 0, tiled=True)
    return settle(place, received, width)


def solution(mesh):
    grid = Mesh(mesh.devices.reshape(tuple(AXES.values())), tuple(AXES))
    rows = P(("y", "core", "x", "z"), None)
    in_specs = (rows, P(), P(None, ("x", "z")), P(("y", "core")), P(("y", "core")))
    return jax.shard_map(shards, mesh=grid, in_specs=in_specs, out_specs=rows, check_vma=False)
```

```python
import jax
import jax.numpy as jnp
from jax import lax
from jax.experimental import pallas as pl
from jax.experimental.pallas import tpu as pltpu
from jax.sharding import Mesh
from jax.sharding import PartitionSpec as P

AXES = {"x": 4, "z": 8, "y": 8, "core": 2}
PAD = 80
MIB = 1024 * 1024
TINY = pl.CostEstimate(flops=0, bytes_accessed=1024, transcendentals=0)


def hop(value, axes, move):
    sizes = [AXES[a] for a in axes]
    total = 1
    for s in sizes:
        total *= s
    pairs = []
    for source in range(total):
        rest, at = source, []
        for s in reversed(sizes):
            at.append(rest % s)
            rest //= s
        target = 0
        for s, c in zip(sizes, move(*reversed(at))):
            target = target * s + c % s
        pairs.append((source, target))
    return lax.ppermute(value, tuple(axes), pairs)


def along_z(value):
    return hop(value, ("z", "core"), lambda z, c: (z + 1 - 2 * c, c))


def along_y(value):
    return hop(value, ("y", "core"), lambda y, c: (y + 1 - 2 * c, c))


def along_x(value):
    return hop(value, ("x", "core"), lambda x, c: (x + 1 - 2 * c, c))


def other_core(value):
    return hop(value, ("core",), lambda c: (1 - c,))


def after(value, *others):
    return lax.optimization_barrier((value, *others))[0]


def mark(*seen):
    def body(*refs):
        refs[-1][...] = jnp.zeros_like(refs[-1])

    return pl.pallas_call(
        body,
        out_shape=jax.ShapeDtypeStruct((8, 128), jnp.float32),
        in_specs=[pl.BlockSpec(memory_space=pltpu.VMEM)] * len(seen),
        out_specs=pl.BlockSpec(memory_space=pltpu.VMEM),
        compiler_params=pltpu.CompilerParams(has_side_effects=True, vmem_limit_bytes=8 * MIB),
        cost_estimate=pl.CostEstimate(flops=10**11, bytes_accessed=1024, transcendentals=0),
        name="mark",
    )(*seen)


def normalize(place, layer_rows, norm_gain, req_len, req_rank):
    rows, features = layer_rows.shape

    def body(place_ref, rows_ref, gain_ref, len_ref, rank_ref, out):
        owned = jnp.where(rank_ref[...] == place_ref[4], len_ref[...], 0)
        live = lax.broadcasted_iota(jnp.int32, (rows, 1), 0) < jnp.sum(owned, axis=1, keepdims=True)
        wide = rows_ref[...].astype(jnp.float32)
        mean_square = jnp.mean(wide * wide, axis=-1, keepdims=True)
        scaled = wide * lax.rsqrt(mean_square + 1e-06) * gain_ref[...]
        out[...] = jnp.where(live, scaled, 0.0).astype(jnp.bfloat16)

    in_vmem = pl.BlockSpec(memory_space=pltpu.VMEM)
    return pl.pallas_call(
        body,
        out_shape=jax.ShapeDtypeStruct((rows, features), jnp.bfloat16),
        in_specs=[pl.BlockSpec(memory_space=pltpu.SMEM)] + [in_vmem] * 4,
        out_specs=in_vmem,
        compiler_params=pltpu.CompilerParams(vmem_limit_bytes=8 * MIB),
        cost_estimate=TINY,
        name="normalize",
    )(place, layer_rows, norm_gain.reshape(1, -1), req_len.reshape(1, -1), req_rank.reshape(1, -1))


def pair_up(one, other):
    rows, features = one.shape

    def body(one_ref, other_ref, out):
        out[0] = one_ref[...]
        out[1] = other_ref[...]

    return pl.pallas_call(
        body,
        out_shape=jax.ShapeDtypeStruct((2, rows, features), one.dtype),
        in_specs=[pl.BlockSpec(memory_space=pltpu.VMEM)] * 2,
        out_specs=pl.BlockSpec(memory_space=pltpu.VMEM),
        compiler_params=pltpu.CompilerParams(vmem_limit_bytes=8 * MIB),
        cost_estimate=TINY,
        name="pair_up",
    )(one, other)


def line_up(place, pair, beside, distant, swapped):
    rows, features = pair.shape[1:]

    def body(place_ref, pair_ref, beside_ref, distant_ref, swapped_ref, out):
        x, c = place_ref[0], place_ref[1]
        back = 2 * c - 1

        def put(step, core, block):
            owner = lax.rem(x + step + 4, 4) * 2 + core
            out[pl.ds(pl.multiple_of(owner * PAD, 16), rows), :] = block

        put(0, c, pair_ref[0])
        put(0, 1 - c, pair_ref[1])
        put(back, c, beside_ref[0])
        put(back, 1 - c, beside_ref[1])
        put(2, c, distant_ref[0])
        put(-back, 1 - c, swapped_ref[0])
        put(-back, c, swapped_ref[1])
        put(2, 1 - c, swapped_ref[2])

    return pl.pallas_call(
        body,
        out_shape=jax.ShapeDtypeStruct((8 * PAD, features), pair.dtype),
        in_specs=[pl.BlockSpec(memory_space=pltpu.SMEM)] + [pl.BlockSpec(memory_space=pltpu.VMEM)] * 4,
        out_specs=pl.BlockSpec(memory_space=pltpu.VMEM),
        compiler_params=pltpu.CompilerParams(vmem_limit_bytes=12 * MIB),
        cost_estimate=TINY,
        name="line_up",
    )(place, pair, beside, distant, swapped)


def project(place, rows_in, near, far, rows, columns, start, lead, into=None):
    total, features = rows_in.shape
    half = features // 2
    owners = total // PAD
    given = list(near) + [w for w in far if w is not None]
    end = start + lead + sum(w.shape[0] for w in near)
    span = columns if into is None else -(-end // 128) * 128
    per = 4
    block = per * PAD

    def body(place_ref, a_ref, *refs):
        out, rest = refs[-1], list(refs[len(near) : len(given)])
        q = place_ref[2]
        first = pl.multiple_of(q * half, 128)
        second = pl.multiple_of((1 - q) * half, 128)
        here = pl.ds(pl.multiple_of(pl.program_id(0) * block, 16), block)
        a_first, a_second = a_ref[here, pl.ds(first, half)], a_ref[here, pl.ds(second, half)]
        w_first, w_second = [], []
        for ref, other in zip(refs[: len(near)], far):
            if other is None:
                w_first.append(ref[:, pl.ds(first, half)])
                w_second.append(ref[:, pl.ds(second, half)])
            else:
                w_first.append(ref[...])
                w_second.append(rest.pop(0)[...])
        if lead:
            w_first.insert(0, w_first[0][:lead])
            w_second.insert(0, w_second[0][:lead])
        contract = (((1,), (1,)), ((), ()))
        gate = lax.dot_general(a_first, jnp.concatenate(w_first, 0), contract, preferred_element_type=jnp.float32)
        gate += lax.dot_general(a_second, jnp.concatenate(w_second, 0), contract, preferred_element_type=jnp.float32)
        act = (gate / (1.0 + jnp.exp(-gate))).astype(jnp.bfloat16)
        if into is not None:
            out[...] = refs[len(given)][...]
        for i in range(per):
            out[i, :, start:end] = act[i * PAD : i * PAD + rows]

    whole = pl.BlockSpec(memory_space=pltpu.VMEM)
    part = pl.BlockSpec((per, rows, span), lambda i: (i, 0, 0))
    kept = [] if into is None else [into]
    return pl.pallas_call(
        body,
        grid=(owners // per,),
        out_shape=jax.ShapeDtypeStruct((owners, rows, columns), jnp.bfloat16),
        in_specs=[pl.BlockSpec(memory_space=pltpu.SMEM)] + [whole] * (1 + len(given)) + [part] * len(kept),
        out_specs=part,
        input_output_aliases={2 + len(given): 0} if kept else {},
        compiler_params=pltpu.CompilerParams(vmem_limit_bytes=20 * MIB),
        cost_estimate=TINY,
        name="project",
    )(place, rows_in, *given, *kept)


def settle(place, received, width):
    rows = received.shape[1]
    half = width // 2
    region = 8 * width

    def body(place_ref, ref, out):
        z = place_ref[3]

        def take(core, k, n=1):
            return ref[core, :, k * half : (k + n) * half]

        parts = [take(0, 1, 2), take(0, 6, 2), take(0, 4, 2), take(0, 3), take(1, 3)]
        for k in (4, 6, 1):
            parts += [take(1, k + 1), take(1, k)]
        parts += [take(0, 0), take(1, 0)]
        line = jnp.concatenate([p.astype(jnp.float32) for p in parts], axis=1)
        line = pltpu.roll(line, lax.rem(z + 5, 8) * width, 1)
        out[...] = line.astype(jnp.bfloat16)

    return pl.pallas_call(
        body,
        grid=(4,),
        out_shape=jax.ShapeDtypeStruct((rows, 4 * region), jnp.bfloat16),
        in_specs=[
            pl.BlockSpec(memory_space=pltpu.SMEM),
            pl.BlockSpec((2, rows, received.shape[2]), lambda i: (i, 0, 0)),
        ],
        out_specs=pl.BlockSpec((rows, region), lambda i: (0, i)),
        compiler_params=pltpu.CompilerParams(vmem_limit_bytes=20 * MIB),
        cost_estimate=TINY,
        name="settle",
    )(place, received)


def shards(layer_rows, norm_gain, w_gate, req_len, req_rank):
    x, z, y, c = (lax.axis_index(a) for a in ("x", "z", "y", "core"))
    rows, features = layer_rows.shape
    width = w_gate.shape[1]
    half_width, half = width // 2, features // 2
    plane = lax.rem(y, 2)
    place = jnp.stack([x, c, plane, z, x * AXES["z"] + z]).astype(jnp.int32)

    weights = w_gate.T

    def own(core):
        return lax.dynamic_slice(weights, (core * half_width, plane * half), (half_width, half))

    a, b = [own(c)], [own(1 - c)]
    a.append(along_z(a[0]))
    b.append(along_z(b[0]))
    normed = normalize(place, layer_rows, after(norm_gain, a[0]), req_len, req_rank)
    pair = pair_up(normed, other_core(normed))
    beside = along_x(pair)

    a.append(along_z(a[1]))
    point = mark(a[1])
    b[1] = after(b[1], point)
    b.append(along_z(b[1]))
    near = [jnp.concatenate([a[1], b[1]], 0)]
    far = [along_y(near[0])]

    a.append(along_z(a[2]))
    point = mark(point, a[2], beside)
    distant = along_x(after(beside[:1], point))
    b[2] = after(b[2], point)
    b.append(along_z(b[2]))
    near.append(jnp.concatenate([a[2], b[2]], 0))
    far.append(along_y(near[1]))

    a.append(along_z(a[3]))
    point = mark(point, a[3], distant, far[0])
    swapped = other_core(after(jnp.concatenate([beside, distant], 0), point))
    near += [a[3], b[3]]
    far += [along_y(after(a[3], point)), along_y(after(b[3], point))]

    near.append(a[4])
    far.append(along_y(a[4]))
    point = mark(point, a[4], far[1])
    rows_in = line_up(place, pair, beside, after(distant, point), swapped)

    own_half = lax.dynamic_slice(weights, (c * half_width, 0), (half_width, features))
    columns = 4 * width
    begin = half_width * 3 // 128 * 128
    gate = project(
        place, rows_in, [own_half] + near[:2], [None] + far[:2], rows, columns, begin, half_width * 3 - begin
    )
    begin = half_width // 128 * 128
    gate = project(place, rows_in, near[2:4], far[2:4], rows, columns, begin, half_width - begin, gate)
    gate = project(place, rows_in, near[4:], far[4:], rows, columns, 0, 0, gate)
    received = lax.all_to_all(gate, ("x", "core"), 0, 0, tiled=True)
    return settle(place, received, width)


def solution(mesh):
    grid = Mesh(mesh.devices.reshape(tuple(AXES.values())), tuple(AXES))
    rows = P(("y", "core", "x", "z"), None)
    in_specs = (rows, P(), P(None, ("x", "z")), P(("y", "core")), P(("y", "core")))
    return jax.shard_map(shards, mesh=grid, in_specs=in_specs, out_specs=rows, check_vma=False)
```

```python
import jax
import jax.numpy as jnp
from jax import lax
from jax.experimental import pallas as pl
from jax.experimental.pallas import tpu as pltpu
from jax.sharding import Mesh
from jax.sharding import PartitionSpec as P

AXES = {"x": 4, "z": 8, "y": 8, "core": 2}
PAD = 80
MIB = 1024 * 1024
TINY = pl.CostEstimate(flops=0, bytes_accessed=1024, transcendentals=0)


def hop(value, axes, move):
    sizes = [AXES[a] for a in axes]
    total = 1
    for s in sizes:
        total *= s
    pairs = []
    for source in range(total):
        rest, at = source, []
        for s in reversed(sizes):
            at.append(rest % s)
            rest //= s
        target = 0
        for s, c in zip(sizes, move(*reversed(at))):
            target = target * s + c % s
        pairs.append((source, target))
    return lax.ppermute(value, tuple(axes), pairs)


def along_z(value):
    return hop(value, ("z", "core"), lambda z, c: (z + 1 - 2 * c, c))


def along_y(value):
    return hop(value, ("y", "core"), lambda y, c: (y + 1 - 2 * c, c))


def along_x(value):
    return hop(value, ("x", "core"), lambda x, c: (x + 1 - 2 * c, c))


def other_core(value):
    return hop(value, ("core",), lambda c: (1 - c,))


def after(value, *others):
    return lax.optimization_barrier((value, *others))[0]


def mark(*seen):
    def body(*refs):
        refs[-1][...] = jnp.zeros_like(refs[-1])

    return pl.pallas_call(
        body,
        out_shape=jax.ShapeDtypeStruct((8, 128), jnp.float32),
        in_specs=[pl.BlockSpec(memory_space=pltpu.VMEM)] * len(seen),
        out_specs=pl.BlockSpec(memory_space=pltpu.VMEM),
        compiler_params=pltpu.CompilerParams(has_side_effects=True, vmem_limit_bytes=8 * MIB),
        cost_estimate=pl.CostEstimate(flops=int(2e10), bytes_accessed=1024, transcendentals=0),
        name="mark",
    )(*seen)


def normalize(place, layer_rows, norm_gain, req_len, req_rank):
    rows, features = layer_rows.shape

    def body(place_ref, rows_ref, gain_ref, len_ref, rank_ref, out):
        owned = jnp.where(rank_ref[...] == place_ref[4], len_ref[...], 0)
        live = lax.broadcasted_iota(jnp.int32, (rows, 1), 0) < jnp.sum(owned, axis=1, keepdims=True)
        wide = rows_ref[...].astype(jnp.float32)
        mean_square = jnp.mean(wide * wide, axis=-1, keepdims=True)
        scaled = wide * lax.rsqrt(mean_square + 1e-06) * gain_ref[...]
        out[...] = jnp.where(live, scaled, 0.0).astype(jnp.bfloat16)

    in_vmem = pl.BlockSpec(memory_space=pltpu.VMEM)
    return pl.pallas_call(
        body,
        out_shape=jax.ShapeDtypeStruct((rows, features), jnp.bfloat16),
        in_specs=[pl.BlockSpec(memory_space=pltpu.SMEM)] + [in_vmem] * 4,
        out_specs=in_vmem,
        compiler_params=pltpu.CompilerParams(vmem_limit_bytes=8 * MIB),
        cost_estimate=TINY,
        name="normalize",
    )(place, layer_rows, norm_gain.reshape(1, -1), req_len.reshape(1, -1), req_rank.reshape(1, -1))


def pair_up(one, other):
    rows, features = one.shape

    def body(one_ref, other_ref, out):
        out[0] = one_ref[...]
        out[1] = other_ref[...]

    return pl.pallas_call(
        body,
        out_shape=jax.ShapeDtypeStruct((2, rows, features), one.dtype),
        in_specs=[pl.BlockSpec(memory_space=pltpu.VMEM)] * 2,
        out_specs=pl.BlockSpec(memory_space=pltpu.VMEM),
        compiler_params=pltpu.CompilerParams(vmem_limit_bytes=8 * MIB),
        cost_estimate=TINY,
        name="pair_up",
    )(one, other)


def line_up(place, pair, beside, distant, swapped):
    rows, features = pair.shape[1:]

    def body(place_ref, pair_ref, beside_ref, distant_ref, swapped_ref, out):
        x, c = place_ref[0], place_ref[1]
        back = 2 * c - 1

        def put(step, core, block):
            owner = lax.rem(x + step + 4, 4) * 2 + core
            out[pl.ds(pl.multiple_of(owner * PAD, 16), rows), :] = block

        put(0, c, pair_ref[0])
        put(0, 1 - c, pair_ref[1])
        put(back, c, beside_ref[0])
        put(back, 1 - c, beside_ref[1])
        put(2, c, distant_ref[0])
        put(-back, 1 - c, swapped_ref[0])
        put(-back, c, swapped_ref[1])
        put(2, 1 - c, swapped_ref[2])

    return pl.pallas_call(
        body,
        out_shape=jax.ShapeDtypeStruct((8 * PAD, features), pair.dtype),
        in_specs=[pl.BlockSpec(memory_space=pltpu.SMEM)] + [pl.BlockSpec(memory_space=pltpu.VMEM)] * 4,
        out_specs=pl.BlockSpec(memory_space=pltpu.VMEM),
        compiler_params=pltpu.CompilerParams(vmem_limit_bytes=12 * MIB),
        cost_estimate=TINY,
        name="line_up",
    )(place, pair, beside, distant, swapped)


def project(place, rows_in, near, far, rows, columns, start, lead, into=None):
    total, features = rows_in.shape
    half = features // 2
    owners = total // PAD
    given = list(near) + [w for w in far if w is not None]
    end = start + lead + sum(w.shape[0] for w in near)
    span = columns if into is None else -(-end // 128) * 128
    per = 4
    block = per * PAD

    def body(place_ref, a_ref, *refs):
        out, rest = refs[-1], list(refs[len(near) : len(given)])
        q = place_ref[2]
        first = pl.multiple_of(q * half, 128)
        second = pl.multiple_of((1 - q) * half, 128)
        here = pl.ds(pl.multiple_of(pl.program_id(0) * block, 16), block)
        a_first, a_second = a_ref[here, pl.ds(first, half)], a_ref[here, pl.ds(second, half)]
        w_first, w_second = [], []
        for ref, other in zip(refs[: len(near)], far):
            if other is None:
                w_first.append(ref[:, pl.ds(first, half)])
                w_second.append(ref[:, pl.ds(second, half)])
            else:
                w_first.append(ref[...])
                w_second.append(rest.pop(0)[...])
        if lead:
            w_first.insert(0, w_first[0][:lead])
            w_second.insert(0, w_second[0][:lead])
        contract = (((1,), (1,)), ((), ()))
        gate = lax.dot_general(a_first, jnp.concatenate(w_first, 0), contract, preferred_element_type=jnp.float32)
        gate += lax.dot_general(a_second, jnp.concatenate(w_second, 0), contract, preferred_element_type=jnp.float32)
        act = (gate / (1.0 + jnp.exp(-gate))).astype(jnp.bfloat16)
        if into is not None:
            out[...] = refs[len(given)][...]
        for i in range(per):
            out[i, :, start:end] = act[i * PAD : i * PAD + rows]

    whole = pl.BlockSpec(memory_space=pltpu.VMEM)
    part = pl.BlockSpec((per, rows, span), lambda i: (i, 0, 0))
    kept = [] if into is None else [into]
    return pl.pallas_call(
        body,
        grid=(owners // per,),
        out_shape=jax.ShapeDtypeStruct((owners, rows, columns), jnp.bfloat16),
        in_specs=[pl.BlockSpec(memory_space=pltpu.SMEM)] + [whole] * (1 + len(given)) + [part] * len(kept),
        out_specs=part,
        input_output_aliases={2 + len(given): 0} if kept else {},
        compiler_params=pltpu.CompilerParams(vmem_limit_bytes=20 * MIB),
        cost_estimate=TINY,
        name="project",
    )(place, rows_in, *given, *kept)


def settle(place, received, width):
    rows = received.shape[1]
    half = width // 2
    region = 8 * width

    def body(place_ref, ref, out):
        z = place_ref[3]

        def take(core, k, n=1):
            return ref[core, :, k * half : (k + n) * half]

        parts = [take(0, 1, 2), take(0, 6, 2), take(0, 4, 2), take(0, 3), take(1, 3)]
        for k in (4, 6, 1):
            parts += [take(1, k + 1), take(1, k)]
        parts += [take(0, 0), take(1, 0)]
        line = jnp.concatenate([p.astype(jnp.float32) for p in parts], axis=1)
        line = pltpu.roll(line, lax.rem(z + 5, 8) * width, 1)
        out[...] = line.astype(jnp.bfloat16)

    return pl.pallas_call(
        body,
        grid=(4,),
        out_shape=jax.ShapeDtypeStruct((rows, 4 * region), jnp.bfloat16),
        in_specs=[
            pl.BlockSpec(memory_space=pltpu.SMEM),
            pl.BlockSpec((2, rows, received.shape[2]), lambda i: (i, 0, 0)),
        ],
        out_specs=pl.BlockSpec((rows, region), lambda i: (0, i)),
        compiler_params=pltpu.CompilerParams(vmem_limit_bytes=20 * MIB),
        cost_estimate=TINY,
        name="settle",
    )(place, received)


def shards(layer_rows, norm_gain, w_gate, req_len, req_rank):
    x, z, y, c = (lax.axis_index(a) for a in ("x", "z", "y", "core"))
    rows, features = layer_rows.shape
    width = w_gate.shape[1]
    half_width, half = width // 2, features // 2
    plane = lax.rem(y, 2)
    place = jnp.stack([x, c, plane, z, x * AXES["z"] + z]).astype(jnp.int32)

    weights = w_gate.T

    def own(core):
        return lax.dynamic_slice(weights, (core * half_width, plane * half), (half_width, half))

    a, b = [own(c)], [own(1 - c)]
    a.append(along_z(a[0]))
    b.append(along_z(b[0]))
    normed = normalize(place, layer_rows, after(norm_gain, a[0]), req_len, req_rank)
    pair = pair_up(normed, other_core(normed))
    beside = along_x(pair)

    a.append(along_z(a[1]))
    point = mark(a[1])
    b[1] = after(b[1], point)
    b.append(along_z(b[1]))
    near = [jnp.concatenate([a[1], b[1]], 0)]
    far = [along_y(near[0])]

    a.append(along_z(a[2]))
    point = mark(point, a[2], beside)
    distant = along_x(after(beside[:1], point))
    b[2] = after(b[2], point)
    near.append(jnp.concatenate([a[2], b[2]], 0))
    far.append(along_y(near[1]))
    point = mark(point, b[2][:16, :128])
    b.append(along_z(after(b[2], point)))

    a.append(along_z(a[3]))
    point = mark(point, a[3], distant, far[0])
    swapped = other_core(after(jnp.concatenate([beside, distant], 0), point))
    near += [a[3], b[3]]
    far += [along_y(after(a[3], point)), along_y(after(b[3], point))]

    near.append(a[4])
    far.append(along_y(a[4]))
    point = mark(point, a[4], far[1])
    rows_in = line_up(place, pair, beside, after(distant, point), swapped)

    later = point[0, 0].astype(jnp.int32)
    own_half = lax.dynamic_slice(weights, (c * half_width + later, 0), (half_width, features))
    columns = 4 * width
    begin = half_width * 3 // 128 * 128
    gate = project(
        place, rows_in, [own_half] + near[:2], [None] + far[:2], rows, columns, begin, half_width * 3 - begin
    )
    begin = half_width // 128 * 128
    gate = project(place, rows_in, near[2:4], far[2:4], rows, columns, begin, half_width - begin, gate)
    gate = project(place, rows_in, near[4:], far[4:], rows, columns, 0, 0, gate)
    received = lax.all_to_all(gate, ("x", "core"), 0, 0, tiled=True)
    return settle(place, received, width)


def solution(mesh):
    grid = Mesh(mesh.devices.reshape(tuple(AXES.values())), tuple(AXES))
    rows = P(("y", "core", "x", "z"), None)
    in_specs = (rows, P(), P(None, ("x", "z")), P(("y", "core")), P(("y", "core")))
    return jax.shard_map(shards, mesh=grid, in_specs=in_specs, out_specs=rows, check_vma=False)
```

```python
import jax
import jax.numpy as jnp
from jax import lax
from jax.experimental import pallas as pl
from jax.experimental.pallas import tpu as pltpu
from jax.sharding import Mesh
from jax.sharding import PartitionSpec as P

AXES = {"x": 4, "z": 8, "y": 8, "core": 2}
PAD = 80
MIB = 1024 * 1024
TINY = pl.CostEstimate(flops=0, bytes_accessed=1024, transcendentals=0)


def hop(value, axes, move):
    sizes = [AXES[a] for a in axes]
    total = 1
    for s in sizes:
        total *= s
    pairs = []
    for source in range(total):
        rest, at = source, []
        for s in reversed(sizes):
            at.append(rest % s)
            rest //= s
        target = 0
        for s, c in zip(sizes, move(*reversed(at))):
            target = target * s + c % s
        pairs.append((source, target))
    return lax.ppermute(value, tuple(axes), pairs)


def along_z(value):
    return hop(value, ("z", "core"), lambda z, c: (z + 1 - 2 * c, c))


def along_y(value):
    return hop(value, ("y", "core"), lambda y, c: (y + 1 - 2 * c, c))


def along_x(value):
    return hop(value, ("x", "core"), lambda x, c: (x + 1 - 2 * c, c))


def other_core(value):
    return hop(value, ("core",), lambda c: (1 - c,))


def after(value, *others):
    return lax.optimization_barrier((value, *others))[0]


def mark(*seen):
    def body(*refs):
        refs[-1][...] = jnp.zeros_like(refs[-1])

    return pl.pallas_call(
        body,
        out_shape=jax.ShapeDtypeStruct((8, 128), jnp.float32),
        in_specs=[pl.BlockSpec(memory_space=pltpu.VMEM)] * len(seen),
        out_specs=pl.BlockSpec(memory_space=pltpu.VMEM),
        compiler_params=pltpu.CompilerParams(has_side_effects=True, vmem_limit_bytes=8 * MIB),
        cost_estimate=pl.CostEstimate(flops=12 * 10**9, bytes_accessed=1024, transcendentals=0),
        name="mark",
    )(*seen)


def normalize(place, layer_rows, norm_gain, req_len, req_rank):
    rows, features = layer_rows.shape

    def body(place_ref, rows_ref, gain_ref, len_ref, rank_ref, out):
        owned = jnp.where(rank_ref[...] == place_ref[4], len_ref[...], 0)
        live = lax.broadcasted_iota(jnp.int32, (rows, 1), 0) < jnp.sum(owned, axis=1, keepdims=True)
        wide = rows_ref[...].astype(jnp.float32)
        mean_square = jnp.mean(wide * wide, axis=-1, keepdims=True)
        scaled = wide * lax.rsqrt(mean_square + 1e-06) * gain_ref[...]
        out[...] = jnp.where(live, scaled, 0.0).astype(jnp.bfloat16)

    in_vmem = pl.BlockSpec(memory_space=pltpu.VMEM)
    return pl.pallas_call(
        body,
        out_shape=jax.ShapeDtypeStruct((rows, features), jnp.bfloat16),
        in_specs=[pl.BlockSpec(memory_space=pltpu.SMEM)] + [in_vmem] * 4,
        out_specs=in_vmem,
        compiler_params=pltpu.CompilerParams(vmem_limit_bytes=8 * MIB),
        cost_estimate=TINY,
        name="normalize",
    )(place, layer_rows, norm_gain.reshape(1, -1), req_len.reshape(1, -1), req_rank.reshape(1, -1))


def pair_up(one, other):
    rows, features = one.shape

    def body(one_ref, other_ref, out):
        out[0] = one_ref[...]
        out[1] = other_ref[...]

    return pl.pallas_call(
        body,
        out_shape=jax.ShapeDtypeStruct((2, rows, features), one.dtype),
        in_specs=[pl.BlockSpec(memory_space=pltpu.VMEM)] * 2,
        out_specs=pl.BlockSpec(memory_space=pltpu.VMEM),
        compiler_params=pltpu.CompilerParams(vmem_limit_bytes=8 * MIB),
        cost_estimate=TINY,
        name="pair_up",
    )(one, other)


def line_up(place, pair, beside, distant, swapped):
    rows, features = pair.shape[1:]

    def body(place_ref, pair_ref, beside_ref, distant_ref, swapped_ref, out):
        x, c = place_ref[0], place_ref[1]
        back = 2 * c - 1

        def put(step, core, block):
            owner = lax.rem(x + step + 4, 4) * 2 + core
            out[pl.ds(pl.multiple_of(owner * PAD, 16), rows), :] = block

        put(0, c, pair_ref[0])
        put(0, 1 - c, pair_ref[1])
        put(back, c, beside_ref[0])
        put(back, 1 - c, beside_ref[1])
        put(2, c, distant_ref[0])
        put(-back, 1 - c, swapped_ref[0])
        put(-back, c, swapped_ref[1])
        put(2, 1 - c, swapped_ref[2])

    return pl.pallas_call(
        body,
        out_shape=jax.ShapeDtypeStruct((8 * PAD, features), pair.dtype),
        in_specs=[pl.BlockSpec(memory_space=pltpu.SMEM)] + [pl.BlockSpec(memory_space=pltpu.VMEM)] * 4,
        out_specs=pl.BlockSpec(memory_space=pltpu.VMEM),
        compiler_params=pltpu.CompilerParams(vmem_limit_bytes=12 * MIB),
        cost_estimate=TINY,
        name="line_up",
    )(place, pair, beside, distant, swapped)


def project(place, rows_in, near, far, rows, columns, start, lead, into=None):
    total, features = rows_in.shape
    half = features // 2
    owners = total // PAD
    given = list(near) + [w for w in far if w is not None]
    end = start + lead + sum(w.shape[0] for w in near)
    span = columns if into is None else -(-end // 128) * 128
    per = 4
    block = per * PAD

    def body(place_ref, a_ref, *refs):
        out, rest = refs[-1], list(refs[len(near) : len(given)])
        q = place_ref[2]
        first = pl.multiple_of(q * half, 128)
        second = pl.multiple_of((1 - q) * half, 128)
        here = pl.ds(pl.multiple_of(pl.program_id(0) * block, 16), block)
        a_first, a_second = a_ref[here, pl.ds(first, half)], a_ref[here, pl.ds(second, half)]
        w_first, w_second = [], []
        for ref, other in zip(refs[: len(near)], far):
            if other is None:
                w_first.append(ref[:, pl.ds(first, half)])
                w_second.append(ref[:, pl.ds(second, half)])
            else:
                w_first.append(ref[...])
                w_second.append(rest.pop(0)[...])
        if lead:
            w_first.insert(0, w_first[0][:lead])
            w_second.insert(0, w_second[0][:lead])
        contract = (((1,), (1,)), ((), ()))
        gate = lax.dot_general(a_first, jnp.concatenate(w_first, 0), contract, preferred_element_type=jnp.float32)
        gate += lax.dot_general(a_second, jnp.concatenate(w_second, 0), contract, preferred_element_type=jnp.float32)
        act = (gate / (1.0 + jnp.exp(-gate))).astype(jnp.bfloat16)
        if into is not None:
            out[...] = refs[len(given)][...]
        for i in range(per):
            out[i, :, start:end] = act[i * PAD : i * PAD + rows]

    whole = pl.BlockSpec(memory_space=pltpu.VMEM)
    part = pl.BlockSpec((per, rows, span), lambda i: (i, 0, 0))
    kept = [] if into is None else [into]
    return pl.pallas_call(
        body,
        grid=(owners // per,),
        out_shape=jax.ShapeDtypeStruct((owners, rows, columns), jnp.bfloat16),
        in_specs=[pl.BlockSpec(memory_space=pltpu.SMEM)] + [whole] * (1 + len(given)) + [part] * len(kept),
        out_specs=part,
        input_output_aliases={2 + len(given): 0} if kept else {},
        compiler_params=pltpu.CompilerParams(vmem_limit_bytes=20 * MIB),
        cost_estimate=TINY,
        name="project",
    )(place, rows_in, *given, *kept)


def settle(place, received, width):
    rows = received.shape[1]
    half = width // 2
    region = 8 * width

    def body(place_ref, ref, out):
        z = place_ref[3]

        def take(core, k, n=1):
            return ref[core, :, k * half : (k + n) * half]

        parts = [take(0, 1, 2), take(0, 6, 2), take(0, 4, 2), take(0, 3), take(1, 3)]
        for k in (4, 6, 1):
            parts += [take(1, k + 1), take(1, k)]
        parts += [take(0, 0), take(1, 0)]
        line = jnp.concatenate([p.astype(jnp.float32) for p in parts], axis=1)
        line = pltpu.roll(line, lax.rem(z + 5, 8) * width, 1)
        out[...] = line.astype(jnp.bfloat16)

    return pl.pallas_call(
        body,
        grid=(4,),
        out_shape=jax.ShapeDtypeStruct((rows, 4 * region), jnp.bfloat16),
        in_specs=[
            pl.BlockSpec(memory_space=pltpu.SMEM),
            pl.BlockSpec((2, rows, received.shape[2]), lambda i: (i, 0, 0)),
        ],
        out_specs=pl.BlockSpec((rows, region), lambda i: (0, i)),
        compiler_params=pltpu.CompilerParams(vmem_limit_bytes=20 * MIB),
        cost_estimate=TINY,
        name="settle",
    )(place, received)


def shards(layer_rows, norm_gain, w_gate, req_len, req_rank):
    x, z, y, c = (lax.axis_index(a) for a in ("x", "z", "y", "core"))
    rows, features = layer_rows.shape
    width = w_gate.shape[1]
    half_width, half = width // 2, features // 2
    plane = lax.rem(y, 2)
    place = jnp.stack([x, c, plane, z, x * AXES["z"] + z]).astype(jnp.int32)

    weights = w_gate.T

    def own(core):
        return lax.dynamic_slice(weights, (core * half_width, plane * half), (half_width, half))

    a, b = [own(c)], [own(1 - c)]
    a.append(along_z(a[0]))
    b.append(along_z(b[0]))
    normed = normalize(place, layer_rows, after(norm_gain, a[0]), req_len, req_rank)
    pair = pair_up(normed, other_core(normed))
    beside = along_x(pair)

    a.append(along_z(a[1]))
    point = mark(a[1])
    later = point[0, 0].astype(jnp.int32)
    own_half = lax.dynamic_slice(weights, (c * half_width + later, 0), (half_width, features))
    b[1] = after(b[1], point)
    b.append(along_z(b[1]))
    near = [jnp.concatenate([a[1], b[1]], 0)]
    far = [along_y(near[0])]

    a.append(along_z(a[2]))
    point = mark(point, a[2], beside)
    distant = along_x(after(beside[:1], point))
    b[2] = after(b[2], point)
    near.append(jnp.concatenate([a[2], b[2]], 0))
    far.append(along_y(near[1]))
    point = mark(point, b[2][:16, :128])
    b.append(along_z(after(b[2], point)))

    a.append(along_z(a[3]))
    point = mark(point, a[3], distant, far[0])
    swapped = other_core(after(jnp.concatenate([beside, distant], 0), point))
    near += [a[3], b[3]]
    far += [along_y(after(a[3], point)), along_y(after(b[3], point))]

    near.append(a[4])
    far.append(along_y(a[4]))
    point = mark(point, a[4], far[1])
    rows_in = line_up(place, pair, beside, after(distant, point), swapped)

    columns = 4 * width
    begin = half_width * 3 // 128 * 128
    gate = project(
        place, rows_in, [own_half] + near[:2], [None] + far[:2], rows, columns, begin, half_width * 3 - begin
    )
    begin = half_width // 128 * 128
    gate = project(place, rows_in, near[2:4], far[2:4], rows, columns, begin, half_width - begin, gate)
    gate = project(place, rows_in, near[4:], far[4:], rows, columns, 0, 0, gate)
    received = lax.all_to_all(gate, ("x", "core"), 0, 0, tiled=True)
    return settle(place, received, width)


def solution(mesh):
    grid = Mesh(mesh.devices.reshape(tuple(AXES.values())), tuple(AXES))
    rows = P(("y", "core", "x", "z"), None)
    in_specs = (rows, P(), P(None, ("x", "z")), P(("y", "core")), P(("y", "core")))
    return jax.shard_map(shards, mesh=grid, in_specs=in_specs, out_specs=rows, check_vma=False)
```

```python
import jax
import jax.numpy as jnp
from jax import lax
from jax.experimental import pallas as pl
from jax.experimental.pallas import tpu as pltpu
from jax.sharding import Mesh
from jax.sharding import PartitionSpec as P

AXES = {"x": 4, "z": 8, "y": 8, "core": 2}
PAD = 80
MIB = 1024 * 1024
TINY = pl.CostEstimate(flops=0, bytes_accessed=1024, transcendentals=0)


def hop(value, axes, move):
    sizes = [AXES[a] for a in axes]
    total = 1
    for s in sizes:
        total *= s
    pairs = []
    for source in range(total):
        rest, at = source, []
        for s in reversed(sizes):
            at.append(rest % s)
            rest //= s
        target = 0
        for s, c in zip(sizes, move(*reversed(at))):
            target = target * s + c % s
        pairs.append((source, target))
    return lax.ppermute(value, tuple(axes), pairs)


def along_z(value):
    return hop(value, ("z", "core"), lambda z, c: (z + 1 - 2 * c, c))


def along_y(value):
    return hop(value, ("y", "core"), lambda y, c: (y + 1 - 2 * c, c))


def along_x(value):
    return hop(value, ("x", "core"), lambda x, c: (x + 1 - 2 * c, c))


def other_core(value):
    return hop(value, ("core",), lambda c: (1 - c,))


def after(value, *others):
    return lax.optimization_barrier((value, *others))[0]


def mark(*seen):
    def body(*refs):
        refs[-1][...] = jnp.zeros_like(refs[-1])

    return pl.pallas_call(
        body,
        out_shape=jax.ShapeDtypeStruct((8, 128), jnp.float32),
        in_specs=[pl.BlockSpec(memory_space=pltpu.VMEM)] * len(seen),
        out_specs=pl.BlockSpec(memory_space=pltpu.VMEM),
        compiler_params=pltpu.CompilerParams(has_side_effects=True, vmem_limit_bytes=8 * MIB),
        cost_estimate=pl.CostEstimate(flops=14 * 10**9, bytes_accessed=1024, transcendentals=0),
        name="mark",
    )(*seen)


def normalize(place, layer_rows, norm_gain, req_len, req_rank):
    rows, features = layer_rows.shape

    def body(place_ref, rows_ref, gain_ref, len_ref, rank_ref, out):
        owned = jnp.where(rank_ref[...] == place_ref[4], len_ref[...], 0)
        live = lax.broadcasted_iota(jnp.int32, (rows, 1), 0) < jnp.sum(owned, axis=1, keepdims=True)
        wide = rows_ref[...].astype(jnp.float32)
        mean_square = jnp.mean(wide * wide, axis=-1, keepdims=True)
        scaled = wide * lax.rsqrt(mean_square + 1e-06) * gain_ref[...]
        out[...] = jnp.where(live, scaled, 0.0).astype(jnp.bfloat16)

    in_vmem = pl.BlockSpec(memory_space=pltpu.VMEM)
    return pl.pallas_call(
        body,
        out_shape=jax.ShapeDtypeStruct((rows, features), jnp.bfloat16),
        in_specs=[pl.BlockSpec(memory_space=pltpu.SMEM)] + [in_vmem] * 4,
        out_specs=in_vmem,
        compiler_params=pltpu.CompilerParams(vmem_limit_bytes=8 * MIB),
        cost_estimate=TINY,
        name="normalize",
    )(place, layer_rows, norm_gain.reshape(1, -1), req_len.reshape(1, -1), req_rank.reshape(1, -1))


def pair_up(one, other):
    rows, features = one.shape

    def body(one_ref, other_ref, out):
        out[0] = one_ref[...]
        out[1] = other_ref[...]

    return pl.pallas_call(
        body,
        out_shape=jax.ShapeDtypeStruct((2, rows, features), one.dtype),
        in_specs=[pl.BlockSpec(memory_space=pltpu.VMEM)] * 2,
        out_specs=pl.BlockSpec(memory_space=pltpu.VMEM),
        compiler_params=pltpu.CompilerParams(vmem_limit_bytes=8 * MIB),
        cost_estimate=TINY,
        name="pair_up",
    )(one, other)


def line_up(place, pair, beside, distant, swapped):
    rows, features = pair.shape[1:]

    def body(place_ref, pair_ref, beside_ref, distant_ref, swapped_ref, out):
        x, c = place_ref[0], place_ref[1]
        back = 2 * c - 1

        def put(step, core, block):
            owner = lax.rem(x + step + 4, 4) * 2 + core
            out[pl.ds(pl.multiple_of(owner * PAD, 16), rows), :] = block

        put(0, c, pair_ref[0])
        put(0, 1 - c, pair_ref[1])
        put(back, c, beside_ref[0])
        put(back, 1 - c, beside_ref[1])
        put(2, c, distant_ref[0])
        put(-back, 1 - c, swapped_ref[0])
        put(-back, c, swapped_ref[1])
        put(2, 1 - c, swapped_ref[2])

    return pl.pallas_call(
        body,
        out_shape=jax.ShapeDtypeStruct((8 * PAD, features), pair.dtype),
        in_specs=[pl.BlockSpec(memory_space=pltpu.SMEM)] + [pl.BlockSpec(memory_space=pltpu.VMEM)] * 4,
        out_specs=pl.BlockSpec(memory_space=pltpu.VMEM),
        compiler_params=pltpu.CompilerParams(vmem_limit_bytes=12 * MIB),
        cost_estimate=TINY,
        name="line_up",
    )(place, pair, beside, distant, swapped)


def project(place, rows_in, near, far, rows, columns, start, lead, into=None):
    total, features = rows_in.shape
    half = features // 2
    owners = total // PAD
    given = list(near) + [w for w in far if w is not None]
    end = start + lead + sum(w.shape[0] for w in near)
    span = columns if into is None else -(-end // 128) * 128
    per = 4
    block = per * PAD

    def body(place_ref, a_ref, *refs):
        out, rest = refs[-1], list(refs[len(near) : len(given)])
        q = place_ref[2]
        first = pl.multiple_of(q * half, 128)
        second = pl.multiple_of((1 - q) * half, 128)
        here = pl.ds(pl.multiple_of(pl.program_id(0) * block, 16), block)
        a_first, a_second = a_ref[here, pl.ds(first, half)], a_ref[here, pl.ds(second, half)]
        w_first, w_second = [], []
        for ref, other in zip(refs[: len(near)], far):
            if other is None:
                w_first.append(ref[:, pl.ds(first, half)])
                w_second.append(ref[:, pl.ds(second, half)])
            else:
                w_first.append(ref[...])
                w_second.append(rest.pop(0)[...])
        if lead:
            w_first.insert(0, w_first[0][:lead])
            w_second.insert(0, w_second[0][:lead])
        contract = (((1,), (1,)), ((), ()))
        gate = lax.dot_general(a_first, jnp.concatenate(w_first, 0), contract, preferred_element_type=jnp.float32)
        gate += lax.dot_general(a_second, jnp.concatenate(w_second, 0), contract, preferred_element_type=jnp.float32)
        act = (gate / (1.0 + jnp.exp(-gate))).astype(jnp.bfloat16)
        if into is not None:
            out[...] = refs[len(given)][...]
        for i in range(per):
            out[i, :, start:end] = act[i * PAD : i * PAD + rows]

    whole = pl.BlockSpec(memory_space=pltpu.VMEM)
    part = pl.BlockSpec((per, rows, span), lambda i: (i, 0, 0))
    kept = [] if into is None else [into]
    return pl.pallas_call(
        body,
        grid=(owners // per,),
        out_shape=jax.ShapeDtypeStruct((owners, rows, columns), jnp.bfloat16),
        in_specs=[pl.BlockSpec(memory_space=pltpu.SMEM)] + [whole] * (1 + len(given)) + [part] * len(kept),
        out_specs=part,
        input_output_aliases={2 + len(given): 0} if kept else {},
        compiler_params=pltpu.CompilerParams(vmem_limit_bytes=20 * MIB),
        cost_estimate=TINY,
        name="project",
    )(place, rows_in, *given, *kept)


def settle(place, received, width):
    rows = received.shape[1]
    half = width // 2
    region = 8 * width

    def body(place_ref, ref, out):
        z = place_ref[3]

        def take(core, k, n=1):
            return ref[core, :, k * half : (k + n) * half]

        parts = [take(0, 1, 2), take(0, 6, 2), take(0, 4, 2), take(0, 3), take(1, 3)]
        for k in (4, 6, 1):
            parts += [take(1, k + 1), take(1, k)]
        parts += [take(0, 0), take(1, 0)]
        line = jnp.concatenate([p.astype(jnp.float32) for p in parts], axis=1)
        line = pltpu.roll(line, lax.rem(z + 5, 8) * width, 1)
        out[...] = line.astype(jnp.bfloat16)

    return pl.pallas_call(
        body,
        grid=(4,),
        out_shape=jax.ShapeDtypeStruct((rows, 4 * region), jnp.bfloat16),
        in_specs=[
            pl.BlockSpec(memory_space=pltpu.SMEM),
            pl.BlockSpec((2, rows, received.shape[2]), lambda i: (i, 0, 0)),
        ],
        out_specs=pl.BlockSpec((rows, region), lambda i: (0, i)),
        compiler_params=pltpu.CompilerParams(vmem_limit_bytes=20 * MIB),
        cost_estimate=TINY,
        name="settle",
    )(place, received)


def shards(layer_rows, norm_gain, w_gate, req_len, req_rank):
    x, z, y, c = (lax.axis_index(a) for a in ("x", "z", "y", "core"))
    rows, features = layer_rows.shape
    width = w_gate.shape[1]
    half_width, half = width // 2, features // 2
    plane = lax.rem(y, 2)
    place = jnp.stack([x, c, plane, z, x * AXES["z"] + z]).astype(jnp.int32)

    weights = w_gate.T

    def own(core):
        return lax.dynamic_slice(weights, (core * half_width, plane * half), (half_width, half))

    a, b = [own(c)], [own(1 - c)]
    a.append(along_z(a[0]))
    b.append(along_z(b[0]))
    normed = normalize(place, layer_rows, after(norm_gain, a[0]), req_len, req_rank)
    pair = pair_up(normed, other_core(normed))
    beside = along_x(pair)

    a.append(along_z(a[1]))
    point = mark(a[1])
    b[1] = after(b[1], point)
    b.append(along_z(b[1]))
    near = [jnp.concatenate([a[1], b[1]], 0)]
    far = [along_y(near[0])]

    a.append(along_z(a[2]))
    point = mark(point, a[2], beside)
    distant = along_x(after(beside[:1], point))
    b[2] = after(b[2], point)
    near.append(jnp.concatenate([a[2], b[2]], 0))
    far.append(along_y(near[1]))
    point = mark(point, b[2][:16, :128])
    b.append(along_z(after(b[2], point)))

    a.append(along_z(a[3]))
    point = mark(point, a[3], distant, far[0])
    swapped = other_core(after(jnp.concatenate([beside, distant], 0), point))
    near += [a[3], b[3]]
    far += [along_y(after(a[3], point)), along_y(after(b[3], point))]

    near.append(a[4])
    far.append(along_y(a[4]))
    point = mark(point, a[4], far[1])
    rows_in = line_up(place, pair, beside, after(distant, point), swapped)

    own_half = lax.dynamic_slice(weights, (c * half_width, 0), (half_width, features))
    columns = 4 * width
    begin = half_width * 3 // 128 * 128
    gate = project(
        place, rows_in, [own_half] + near[:2], [None] + far[:2], rows, columns, begin, half_width * 3 - begin
    )
    begin = half_width // 128 * 128
    gate = project(place, rows_in, near[2:4], far[2:4], rows, columns, begin, half_width - begin, gate)
    gate = project(place, rows_in, near[4:], far[4:], rows, columns, 0, 0, gate)
    received = lax.all_to_all(gate, ("x", "core"), 0, 0, tiled=True)
    return settle(place, received, width)


def solution(mesh):
    grid = Mesh(mesh.devices.reshape(tuple(AXES.values())), tuple(AXES))
    rows = P(("y", "core", "x", "z"), None)
    in_specs = (rows, P(), P(None, ("x", "z")), P(("y", "core")), P(("y", "core")))
    return jax.shard_map(shards, mesh=grid, in_specs=in_specs, out_specs=rows, check_vma=False)
```
